512 devices in a mesh: snd: 32 (over y, x, core), rcv: 16 (over z).
Axes of the slice: x: 4, y: 4, z: 16, core: 2. Of those that a mesh axis runs over, the one named last changes fastest.
Arguments:
- nodes: bfloat16 [4096, 512], P(('snd', 'rcv')), may hold values from -6 to 6
- edges: bfloat16 [32, 16, 256, 512], P('snd', 'rcv'), may hold values from -6 to 6
- send_local: int32 [32, 16, 256], P('snd', 'rcv'), may hold values from 0 to 127
- recv_local: int32 [32, 16, 256], P('snd', 'rcv'), may hold values from 0 to 255
- edge_count: int32 [32, 16], P('snd', 'rcv'), may hold values from 32 to 256, as said below
- edge_w1: bfloat16 [1536, 512], replicated, may hold values from -0.15625 to 0.15625
- edge_w2: bfloat16 [512, 512], replicated, may hold values from -0.25 to 0.25
- node_w1: bfloat16 [1024, 512], replicated, may hold values from -0.1875 to 0.1875
- node_w2: bfloat16 [512, 512], replicated, may hold values from -0.25 to 0.25
- grad_nodes_out: bfloat16 [4096, 512], P(('snd', 'rcv')), may hold values from -6 to 6
- grad_edges_out: bfloat16 [32, 16, 256, 512], P('snd', 'rcv'), may hold values from -6 to 6
Outputs:
- grad_nodes: float32 [4096, 512], P(('snd', 'rcv'))
- grad_edges: float32 [32, 16, 256, 512], P('snd', 'rcv')
The draws below stay inside these ranges and needn't reach their ends.
Inputs may be any that keep to these rules, and one draw needn't show every extreme that they name: Live edges of a tile fill its first edge_count slots; in every draw some tile has all 256 slots live.
All inputs are finite; a program needn't handle non-finite values.
Results may differ from the reference program's by a relative error of at most 0.019.
Values may be sent and summed in bfloat16 or wider, within the bound.
A program may use at most 64 MiB of HBM per device.

```python
import jax
import jax.numpy as jnp
from jax import lax

D = 512
HID = 512
NODE_DEV = 8
E_DEV = 256
SEND_ROWS = 128
RECV_ROWS = 256
NODES = 4096
N_SND = 32
N_RCV = 16


def draw_edge_count(key, part):
    key = jax.random.fold_in(key, 7)
    key_shift, key_spot = jax.random.split(key)
    shifts = jax.random.randint(key_shift, (N_SND * N_RCV,), 0, 4)
    counts = E_DEV // jnp.left_shift(jnp.ones_like(shifts), shifts)
    spot = jax.random.randint(key_spot, (), 0, N_SND * N_RCV)
    counts = jnp.where(jnp.arange(N_SND * N_RCV, dtype=jnp.int32) == spot, E_DEV, counts)
    return counts.reshape(N_SND, N_RCV).astype(jnp.int32)


def draw_recv_local(key, part):
    key = jax.random.fold_in(key, 11)
    key_mode, key_side, key_offset, key_any = jax.random.split(key, 4)
    shape = (N_SND, N_RCV, E_DEV)
    mode = jax.random.randint(key_mode, shape, 0, 2)
    side = jax.random.randint(key_side, shape, 0, 2)
    offset = jax.random.randint(key_offset, shape, 0, NODE_DEV)
    anywhere = jax.random.randint(key_any, shape, 0, RECV_ROWS)
    group = jax.lax.broadcasted_iota(jnp.int32, shape, 0)
    owner = (group + side * (N_SND // 2)) % N_SND
    nearby = owner * NODE_DEV + offset
    chosen = jnp.where(mode == 0, nearby, anywhere)
    slot = jax.lax.broadcasted_iota(jnp.int32, shape, 2)
    first = (jax.lax.broadcasted_iota(jnp.int32, shape, 0) == 0) & (jax.lax.broadcasted_iota(jnp.int32, shape, 1) == 0)
    chosen = jnp.where(first & (slot == 0), 0, chosen)
    chosen = jnp.where(first & (slot == 1), RECV_ROWS - 1, chosen)
    return chosen.astype(jnp.int32)


def touch_ends(entries, key, low, largest):
    index_at = [jax.random.randint(jax.random.fold_in(key, axis), (), 0, length) for axis, length in enumerate(entries.shape)]
    main_axis = entries.shape.index(max(entries.shape))
    neighbour = index_at[:main_axis] + [(index_at[main_axis] + 1) % entries.shape[main_axis]] + index_at[main_axis + 1:]
    return entries.at[tuple(index_at)].set(low).at[tuple(neighbour)].set(largest)


def levels(rng, extent, cuts, low, largest):
    def one(position, shards_of):
        heights = jax.random.uniform(jax.random.fold_in(jax.random.fold_in(rng, 6), position), (shards_of,), jnp.float32, low / len(cuts), largest / len(cuts))
        return jnp.repeat(jnp.exp(heights), extent[position] // shards_of).reshape((-1,) + (1,) * (len(extent) - position - 1))

    factor_of = one(*cuts[0])
    for cut in cuts[1:]:
        factor_of = factor_of * one(*cut)
    return factor_of


def centred(stream_key, extent, width, reach, cuts=(), kind=jnp.bfloat16):
    array = width * jax.random.normal(stream_key, extent, jnp.float32)
    if cuts:
        array = array * levels(stream_key, extent, cuts, -0.22, 0.18)
    return jnp.clip(array, -reach, reach).astype(kind)


def setup_inputs(seed: int = 0) -> dict:
    key_of = jax.random.split(jax.random.key(seed), 12)
    return {
        "nodes": centred(key_of[0], (NODES, D), 1.0, 6.0, ((0, 512),)),
        "edges": centred(key_of[1], (N_SND, N_RCV, E_DEV, D), 1.0, 6.0, ((0, 32), (1, 16))),
        "send_local": touch_ends(jax.random.randint(key_of[2], (N_SND, N_RCV, E_DEV), 0, SEND_ROWS), jax.random.fold_in(key_of[2], 1), 0, SEND_ROWS - 1).astype(jnp.int32),
        "recv_local": draw_recv_local(jax.random.fold_in(key_of[11], 71), 0),
        "edge_count": draw_edge_count(jax.random.fold_in(key_of[11], 71), 0),
        "edge_w1": centred(key_of[5], (3 * D, HID), (3 * D) ** -0.5, 0.15625),
        "edge_w2": centred(key_of[6], (HID, D), HID ** -0.5, 0.25),
        "node_w1": centred(key_of[7], (2 * D, HID), (2 * D) ** -0.5, 0.1875),
        "node_w2": centred(key_of[8], (HID, D), HID ** -0.5, 0.25),
        "grad_nodes_out": centred(key_of[9], (NODES, D), 1.0, 6.0, ((0, 512),)),
        "grad_edges_out": centred(key_of[10], (N_SND, N_RCV, E_DEV, D), 1.0, 6.0, ((0, 32), (1, 16))),
    }


def swish_slope(pre_act):
    sigma = jax.nn.sigmoid(pre_act)
    return sigma * (1.0 + pre_act * (1.0 - sigma))

def layer_norm(values):
    center = values - lax.optimization_barrier(jnp.mean(values, -1, keepdims=True))
    inv_scale = lax.rsqrt(lax.optimization_barrier(jnp.mean(center * center, -1, keepdims=True)) + 1e-05)
    return (center * inv_scale, inv_scale)

def norm_backward(upstream, normed, inv_scale):
    return inv_scale * (upstream - lax.optimization_barrier(jnp.mean(upstream, -1, keepdims=True)) - normed * lax.optimization_barrier(jnp.mean(upstream * normed, -1, keepdims=True)))

def mlp_forward(inputs_cat, first_w, second_w):
    pre_act = jnp.dot(inputs_cat, first_w, preferred_element_type=jnp.float32)
    hidden = jax.nn.silu(pre_act).astype(jnp.bfloat16)
    output = jnp.dot(hidden, second_w, preferred_element_type=jnp.float32)
    normed, inv_scale = layer_norm(output)
    return (pre_act, normed, inv_scale)

def mlp_backward(upstream, pre_act, normed, inv_scale, first_w, second_w):
    grad_out = norm_backward(upstream, normed, inv_scale).astype(jnp.bfloat16)
    grad_hidden = jnp.dot(grad_out, second_w.T, preferred_element_type=jnp.float32)
    grad_pre = (grad_hidden * swish_slope(pre_act)).astype(jnp.bfloat16)
    return jnp.dot(grad_pre, first_w.T, preferred_element_type=jnp.float32)

def node_backward(node_feat, aggregate, upstream_bf, node_w1, node_w2):
    feat_width = node_feat.shape[1]
    inputs_cat = jnp.concatenate([node_feat, aggregate.astype(jnp.bfloat16)], 1)
    pre_act, normed, inv_scale = mlp_forward(inputs_cat, node_w1, node_w2)
    upstream = upstream_bf.astype(jnp.float32)
    grad_in = mlp_backward(upstream, pre_act, normed, inv_scale, node_w1, node_w2)
    return (upstream + grad_in[:, :feat_width], grad_in[:, feat_width:])

def reference(nodes, edges, send_local, recv_local, edge_count, edge_w1, edge_w2, node_w1, node_w2, grad_nodes_out, grad_edges_out):
    feat_width = nodes.shape[1]
    snd_ids = jnp.arange(N_SND, dtype=jnp.int32)[:, None, None]
    rcv_ids = jnp.arange(N_RCV, dtype=jnp.int32)[None, :, None]
    send_global = snd_ids * (NODE_DEV * N_RCV) + send_local
    recv_global = (recv_local // NODE_DEV * N_RCV + rcv_ids) * NODE_DEV + recv_local % NODE_DEV
    live_mask = (jnp.arange(E_DEV, dtype=jnp.int32)[None, None, :] < edge_count[:, :, None]).astype(jnp.float32)

    def edge_inputs(block):
        joined = jnp.concatenate([edges[block], nodes[send_global[block]], nodes[recv_global[block]]], -1)
        return joined.reshape(-1, 3 * feat_width)

    def forward_pass(agg_sum, block):
        pre_act, normed, inv_scale = mlp_forward(edge_inputs(block), edge_w1, edge_w2)
        block_mask = live_mask[block].reshape(-1, 1)
        agg_sum = agg_sum.at[recv_global[block].reshape(-1)].add(normed * block_mask)
        return (agg_sum, None)
    blocks = jnp.arange(N_SND, dtype=jnp.int32)
    aggregate, _ = lax.scan(forward_pass, jnp.zeros(nodes.shape, jnp.float32), blocks)
    direct, aggregate_grad = node_backward(nodes, aggregate, grad_nodes_out, node_w1, node_w2)

    def backward_pass(grad_sum, block):
        pre_act, normed, inv_scale = mlp_forward(edge_inputs(block), edge_w1, edge_w2)
        block_mask = live_mask[block].reshape(-1, 1)
        send_flat = send_global[block].reshape(-1)
        recv_flat = recv_global[block].reshape(-1)
        cotangent = grad_edges_out[block].reshape(-1, feat_width).astype(jnp.float32)
        upstream = (cotangent + aggregate_grad[recv_flat]) * block_mask
        grad_in = mlp_backward(upstream, pre_act, normed, inv_scale, edge_w1, edge_w2)
        edge_grad = block_mask * cotangent + grad_in[:, :feat_width]
        grad_sum = grad_sum.at[send_flat].add(grad_in[:, feat_width:2 * feat_width])
        grad_sum = grad_sum.at[recv_flat].add(grad_in[:, 2 * feat_width:])
        return (grad_sum, edge_grad.reshape(N_RCV, E_DEV, feat_width))
    node_sum, edge_grads = lax.scan(backward_pass, jnp.zeros(nodes.shape, jnp.float32), blocks)
    return (direct + node_sum, edge_grads)
```

```python
import jax
import jax.numpy as jnp
from jax import lax
from jax.experimental import pallas as pl
from jax.experimental.pallas import tpu as pltpu
from jax.sharding import PartitionSpec as P

MESH = pl.DeviceIdType.MESH
F32 = jnp.float32
BF16 = jnp.bfloat16
CHUNK = 64


def dot(a, b):
    return jnp.dot(a, b, preferred_element_type=F32)


def dot_t(a, b):
    return lax.dot_general(a, b, (((1,), (1,)), ((), ())), preferred_element_type=F32)


def pack_blocks(rows):
    count, width = rows.shape[0] // 8, rows.shape[1]
    blocks = rows.reshape(count, 8, width)
    return jnp.concatenate(
        [blocks[:, :, : width // 2], blocks[:, :, width // 2 :]], axis=1
    ).astype(BF16)


def unpack_blocks(blocks):
    blocks = blocks.astype(F32)
    count, _, half = blocks.shape
    return jnp.concatenate(
        [blocks[:, :8, :].reshape(count * 8, half), blocks[:, 8:, :].reshape(count * 8, half)],
        axis=1,
    )


def unpack_sum(blocks):
    total = jnp.sum(blocks.astype(F32), axis=0)
    return jnp.concatenate([total[:8], total[8:]], axis=1)


def layer_norm(values):
    center = values - jnp.mean(values, -1, keepdims=True)
    inv_scale = lax.rsqrt(jnp.mean(center * center, -1, keepdims=True) + 1e-05)
    return center * inv_scale, inv_scale


def norm_backward(upstream, normed, inv_scale):
    return inv_scale * (
        upstream
        - jnp.mean(upstream, -1, keepdims=True)
        - normed * jnp.mean(upstream * normed, -1, keepdims=True)
    )


def make_kernel(n_snd, n_rcv):
    def kernel(
        count_ref,
        send_ref,
        recv_ref,
        nodes_ref,
        gno_ref,
        edges_hbm,
        geo_hbm,
        w1_hbm,
        w2_hbm,
        nw1_hbm,
        nw2_hbm,
        gnodes_ref,
        gedges_ref,
        edges,
        geo,
        w1,
        w2,
        nw1,
        nw2,
        node_blk,
        nodes_r,
        nodes_s,
        agg_out,
        agg_in,
        gagg_blk,
        gagg_in,
        rs_out,
        rs_in,
        rr_out,
        rr_in,
        pre,
        normed,
        inv,
        work,
        hid,
        slope,
        load_sem,
        send_sem,
        recv_sem,
    ):
        me_s = lax.axis_index("snd")
        me_r = lax.axis_index("rcv")
        n_edges = edges.shape[0]
        d = edges.shape[1]

        loads = [
            pltpu.make_async_copy(src, dst, load_sem.at[k])
            for k, (src, dst) in enumerate(
                [
                    (edges_hbm, edges),
                    (w1_hbm, w1),
                    (w2_hbm, w2),
                    (nw1_hbm, nw1),
                    (nw2_hbm, nw2),
                    (geo_hbm, geo),
                ]
            )
        ]
        for load in loads:
            load.start()

        barrier = pltpu.get_barrier_semaphore()

        def greet(axis, me, n):
            def body(step, carry):
                pl.semaphore_signal(
                    barrier,
                    inc=1,
                    device_id={axis: lax.rem(me + step, n)},
                    device_id_type=MESH,
                )
                return carry

            lax.fori_loop(1, n, body, 0)

        greet("rcv", me_r, n_rcv)
        greet("snd", me_s, n_snd)

        def send_all(axis, me, n, src_of, dst, k):
            def body(step, carry):
                other = lax.rem(me + step, n)
                pltpu.make_async_remote_copy(
                    src_ref=src_of(other),
                    dst_ref=dst.at[me],
                    send_sem=send_sem.at[k],
                    recv_sem=recv_sem.at[k],
                    device_id={axis: other},
                    device_id_type=MESH,
                ).start()
                return carry

            lax.fori_loop(1, n, body, 0)

        def wait_for(sem, buf, n, k):
            part = buf.at[pl.ds(0, n - 1)]
            pltpu.make_async_copy(part, part, sem.at[k]).wait()

        own = pack_blocks(nodes_ref[...].astype(F32))
        node_blk[...] = own[0]
        nodes_r[me_r] = own[0]
        nodes_s[me_s] = own[0]

        pl.semaphore_wait(barrier, n_snd + n_rcv - 2)
        send_all("rcv", me_r, n_rcv, lambda o: node_blk, nodes_r, 0)
        send_all("snd", me_s, n_snd, lambda o: node_blk, nodes_s, 1)

        live_row = lax.broadcasted_iota(jnp.int32, (1, n_edges), 1) < count_ref[0, 0]
        live_col = lax.broadcasted_iota(jnp.int32, (n_edges, 1), 0) < count_ref[0, 0]
        send_idx = jnp.where(live_row, send_ref[...], -1)
        recv_idx = jnp.where(live_row, recv_ref[...], -1)

        def picker(idx, rows):
            rows_iota = lax.broadcasted_iota(jnp.int32, (rows, n_edges), 0)
            return jnp.where(rows_iota == idx, 1.0, 0.0).astype(F32)

        put_s = picker(send_idx, n_rcv * 8)
        put_r = picker(recv_idx, n_snd * 8)
        take_s = put_s.T.astype(BF16)
        take_r = put_r.T.astype(BF16)
        put_s = put_s.astype(BF16)
        put_r = put_r.astype(BF16)

        loads[0].wait()
        loads[1].wait()
        pre[...] = dot(edges[...], w1[:d])

        wait_for(recv_sem, nodes_r, n_rcv, 0)
        sender = dot(take_s, unpack_blocks(nodes_r[...]).astype(BF16)).astype(BF16)
        pre[...] += dot(sender, w1[d : 2 * d])
        wait_for(recv_sem, nodes_s, n_snd, 1)
        receiver = dot(take_r, unpack_blocks(nodes_s[...]).astype(BF16)).astype(BF16)
        work[...] = dot(receiver, w1[2 * d :])
        for start in range(0, n_edges, CHUNK):
            rows = pl.ds(start, CHUNK)
            act = pre[rows] + work[rows]
            pre[rows] = act
            hid[rows] = (act * jax.nn.sigmoid(act)).astype(BF16)
        loads[2].wait()
        work[...] = dot(hid[...], w2[...])
        for start in range(0, n_edges, CHUNK):
            rows = pl.ds(start, CHUNK)
            out, scale = layer_norm(work[rows])
            normed[rows] = out
            inv[rows] = scale
            hid[rows] = out.astype(BF16)
        agg_out[...] = pack_blocks(dot(put_r, hid[...]))
        send_all("snd", me_s, n_snd, lambda o: agg_out.at[o], agg_in, 2)
        agg_in[me_s] = agg_out[me_s]

        loads[3].wait()
        loads[4].wait()
        loads[5].wait()
        node_pre = dot(nodes_ref[...], nw1[:d])
        for start in range(0, n_edges, CHUNK):
            rows = pl.ds(start, CHUNK)
            act = pre[rows]
            sigma = jax.nn.sigmoid(act)
            slope[rows] = sigma * (1.0 + act * (1.0 - sigma))

        wait_for(recv_sem, agg_in, n_snd, 2)
        aggregate = unpack_sum(agg_in[...]).astype(BF16)
        node_pre = node_pre + dot(aggregate, nw1[d:])
        sigma = jax.nn.sigmoid(node_pre)
        node_out = dot((node_pre * sigma).astype(BF16), nw2[...])
        node_normed, node_inv = layer_norm(node_out)
        gno = gno_ref[...].astype(F32)
        node_gout = norm_backward(gno, node_normed, node_inv).astype(BF16)
        node_gpre = (
            dot_t(node_gout, nw2[...]) * (sigma * (1.0 + node_pre * (1.0 - sigma)))
        ).astype(BF16)
        gagg = pack_blocks(dot_t(node_gpre, nw1[d:]))
        gagg_blk[...] = gagg[0]
        gagg_in[me_s] = gagg[0]
        send_all("snd", me_s, n_snd, lambda o: gagg_blk, gagg_in, 3)
        direct = gno + dot_t(node_gpre, nw1[:d])

        wait_for(recv_sem, gagg_in, n_snd, 3)
        work[...] = dot(take_r, unpack_blocks(gagg_in[...]).astype(BF16))
        for start in range(0, n_edges, CHUNK):
            rows = pl.ds(start, CHUNK)
            live = (
                lax.broadcasted_iota(jnp.int32, (CHUNK, 1), 0) + start < count_ref[0, 0]
            )
            up = work[rows] + jnp.where(live, geo[rows].astype(F32), 0.0)
            hid[rows] = norm_backward(up, normed[rows], inv[rows]).astype(BF16)
        work[...] = dot_t(hid[...], w2[...])
        for start in range(0, n_edges, CHUNK):
            rows = pl.ds(start, CHUNK)
            hid[rows] = (work[rows] * slope[rows]).astype(BF16)
        send_part = dot_t(hid[...], w1[d : 2 * d]).astype(BF16)
        rs_out[...] = pack_blocks(dot(put_s, send_part))
        send_all("rcv", me_r, n_rcv, lambda o: rs_out.at[o], rs_in, 4)
        rs_in[me_r] = rs_out[me_r]
        recv_part = dot_t(hid[...], w1[2 * d :]).astype(BF16)
        rr_out[...] = pack_blocks(dot(put_r, recv_part))
        send_all("snd", me_s, n_snd, lambda o: rr_out.at[o], rr_in, 5)
        rr_in[me_s] = rr_out[me_s]
        gedges_ref[...] = jnp.where(live_col, geo[...].astype(F32), 0.0) + dot_t(
            hid[...], w1[:d]
        )

        wait_for(recv_sem, rr_in, n_snd, 5)
        direct = direct + unpack_sum(rr_in[...])
        wait_for(recv_sem, rs_in, n_rcv, 4)
        gnodes_ref[...] = direct + unpack_sum(rs_in[...])

        wait_for(send_sem, nodes_r, n_rcv, 0)
        wait_for(send_sem, nodes_s, n_snd, 1)
        wait_for(send_sem, agg_in, n_snd, 2)
        wait_for(send_sem, gagg_in, n_snd, 3)
        wait_for(send_sem, rs_in, n_rcv, 4)
        wait_for(send_sem, rr_in, n_snd, 5)

    return kernel


def solution(mesh):
    n_snd, n_rcv = mesh.shape["snd"], mesh.shape["rcv"]

    def local(
        nodes,
        edges,
        send_local,
        recv_local,
        edge_count,
        edge_w1,
        edge_w2,
        node_w1,
        node_w2,
        grad_nodes_out,
        grad_edges_out,
    ):
        n_edges, d = edges.shape[2:]
        vmem = pl.BlockSpec(memory_space=pltpu.VMEM)
        hbm = pl.BlockSpec(memory_space=pltpu.HBM)
        smem = pl.BlockSpec(memory_space=pltpu.SMEM)
        half = d // 2
        grad_nodes, grad_edges = pl.pallas_call(
            make_kernel(n_snd, n_rcv),
            out_shape=(
                jax.ShapeDtypeStruct(nodes.shape, F32),
                jax.ShapeDtypeStruct((n_edges, d), F32),
            ),
            in_specs=[smem, vmem, vmem, vmem, vmem] + [hbm] * 6,
            out_specs=(vmem, vmem),
            scratch_shapes=[
                pltpu.VMEM((n_edges, d), BF16),
                pltpu.VMEM((n_edges, d), BF16),
                pltpu.VMEM(edge_w1.shape, BF16),
                pltpu.VMEM(edge_w2.shape, BF16),
                pltpu.VMEM(node_w1.shape, BF16),
                pltpu.VMEM(node_w2.shape, BF16),
                pltpu.VMEM((16, half), BF16),
                pltpu.VMEM((n_rcv, 16, half), BF16),
                pltpu.VMEM((n_snd, 16, half), BF16),
                pltpu.VMEM((n_snd, 16, half), BF16),
                pltpu.VMEM((n_snd, 16, half), BF16),
                pltpu.VMEM((16, half), BF16),
                pltpu.VMEM((n_snd, 16, half), BF16),
                pltpu.VMEM((n_rcv, 16, half), BF16),
                pltpu.VMEM((n_rcv, 16, half), BF16),
                pltpu.VMEM((n_snd, 16, half), BF16),
                pltpu.VMEM((n_snd, 16, half), BF16),
                pltpu.VMEM((n_edges, d), F32),
                pltpu.VMEM((n_edges, d), F32),
                pltpu.VMEM((n_edges, 1), F32),
                pltpu.VMEM((n_edges, d), F32),
                pltpu.VMEM((n_edges, d), BF16),
                pltpu.VMEM((n_edges, d), F32),
                pltpu.SemaphoreType.DMA((6,)),
                pltpu.SemaphoreType.DMA((6,)),
                pltpu.SemaphoreType.DMA((6,)),
            ],
            compiler_params=pltpu.CompilerParams(
                collective_id=0, has_side_effects=True, vmem_limit_bytes=48 * 1024 * 1024
            ),
        )(
            edge_count,
            send_local.reshape(1, n_edges),
            recv_local.reshape(1, n_edges),
            nodes,
            grad_nodes_out,
            edges.reshape(n_edges, d),
            grad_edges_out.reshape(n_edges, d),
            edge_w1,
            edge_w2,
            node_w1,
            node_w2,
        )
        return grad_nodes, grad_edges.reshape(1, 1, n_edges, d)

    in_specs = (
        P(("snd", "rcv"), None),
        P("snd", "rcv", None, None),
        P("snd", "rcv", None),
        P("snd", "rcv", None),
        P("snd", "rcv"),
        P(),
        P(),
        P(),
        P(),
        P(("snd", "rcv"), None),
        P("snd", "rcv", None, None),
    )
    out_specs = (P(("snd", "rcv"), None), P("snd", "rcv", None, None))
    return jax.shard_map(local, mesh=mesh, in_specs=in_specs, out_specs=out_specs, check_vma=False)
```

```python
import itertools

import jax
import jax.numpy as jnp
from jax import lax
from jax.experimental import pallas as pl
from jax.experimental.pallas import tpu as pltpu
from jax.sharding import PartitionSpec as P

MESH = pl.DeviceIdType.MESH
F32 = jnp.float32
BF16 = jnp.bfloat16
CHUNK = 64


def dot(a, b):
    return jnp.dot(a, b, preferred_element_type=F32)


def dot_t(a, b):
    return lax.dot_general(a, b, (((1,), (1,)), ((), ())), preferred_element_type=F32)


def pack_blocks(rows):
    count, width = rows.shape[0] // 8, rows.shape[1]
    blocks = rows.reshape(count, 8, width)
    return jnp.concatenate(
        [blocks[:, :, : width // 2], blocks[:, :, width // 2 :]], axis=1
    ).astype(BF16)


def unpack_blocks(blocks):
    blocks = blocks.astype(F32)
    count, _, half = blocks.shape
    return jnp.concatenate(
        [blocks[:, :8, :].reshape(count * 8, half), blocks[:, 8:, :].reshape(count * 8, half)],
        axis=1,
    )


def unpack_sum(blocks):
    total = jnp.sum(blocks.astype(F32), axis=0)
    return jnp.concatenate([total[:8], total[8:]], axis=1)


def layer_norm(values):
    center = values - jnp.mean(values, -1, keepdims=True)
    inv_scale = lax.rsqrt(jnp.mean(center * center, -1, keepdims=True) + 1e-05)
    return center * inv_scale, inv_scale


def norm_backward(upstream, normed, inv_scale):
    return inv_scale * (
        upstream
        - jnp.mean(upstream, -1, keepdims=True)
        - normed * jnp.mean(upstream * normed, -1, keepdims=True)
    )


def make_kernel(n_snd, n_rcv):
    far_first = sorted(range(1, n_rcv), key=lambda step: -min(step, n_rcv - step))

    def kernel(
        count_hbm,
        send_hbm,
        recv_hbm,
        nodes_hbm,
        gno_hbm,
        edges_hbm,
        geo_hbm,
        w1_hbm,
        w2_hbm,
        nw1_hbm,
        nw2_hbm,
        gnodes_ref,
        gedges_ref,
        count_ref,
        send_ref,
        recv_ref,
        nodes_ref,
        gno_ref,
        edges,
        geo,
        w1,
        w2,
        nw1,
        nw2,
        node_blk,
        nodes_r,
        nodes_s,
        agg_out,
        agg_in,
        gagg_blk,
        gagg_in,
        rs_out,
        rs_in,
        rr_out,
        rr_in,
        pre,
        normed,
        inv,
        work,
        hid,
        slope,
        put_s,
        put_r,
        take_s,
        take_r,
        load_sem,
        send_sem,
        recv_sem,
        plane_sem,
    ):
        me_s = lax.axis_index("snd")
        me_r = lax.axis_index("rcv")
        n_edges = edges.shape[0]
        d = edges.shape[1]

        loads = [
            pltpu.make_async_copy(src, dst, load_sem.at[k])
            for k, (src, dst) in enumerate(
                [
                    (nodes_hbm, nodes_ref),
                    (count_hbm, count_ref),
                    (send_hbm, send_ref),
                    (recv_hbm, recv_ref),
                    (edges_hbm, edges),
                    (w1_hbm, w1),
                    (w2_hbm, w2),
                    (nw1_hbm, nw1),
                    (nw2_hbm, nw2),
                    (geo_hbm, geo),
                    (gno_hbm, gno_ref),
                ]
            )
        ]
        for load in loads:
            load.start()

        barrier = pltpu.get_barrier_semaphore()

        def plane(step):
            return (me_r + step + n_rcv) % n_rcv

        cores = [me_s % 2, (me_s + 1) % 2]
        columns = [(me_s // 2 + dx) % 4 * 2 for dx in range(4)]
        lines = [(me_s // 8 + dy) % 4 * 8 for dy in range(4)]
        snd_partners = [
            lines[dy] + columns[dx] + cores[core]
            for dy, dx, core in sorted(
                itertools.product(range(4), range(4), range(2)),
                key=lambda step: -min(step[0], 4 - step[0]) - min(step[1], 4 - step[1]) - step[2] / 2,
            )[:-1]
        ]

        for other in snd_partners:
            pl.semaphore_signal(barrier, inc=1, device_id={"snd": other}, device_id_type=MESH)

        near = (4, -4, 3, -3, 2, -2, 1, -1)
        for step in near:
            pl.semaphore_signal(
                barrier, inc=1, device_id={"rcv": plane(step)}, device_id_type=MESH
            )

        def copy_snd(other, src, dst, k):
            return pltpu.make_async_remote_copy(
                src_ref=src,
                dst_ref=dst.at[me_s],
                send_sem=send_sem.at[k],
                recv_sem=recv_sem.at[k],
                device_id={"snd": other},
                device_id_type=MESH,
            )

        def send_snd(src_of, dst, k):
            for other in snd_partners:
                copy_snd(other, src_of(other), dst, k).start()

        def send_rcv(src_of, dst, k):
            for step in far_first:
                other = (me_r + step) % n_rcv
                pltpu.make_async_remote_copy(
                    src_ref=src_of(other),
                    dst_ref=dst.at[me_r],
                    send_sem=send_sem.at[k],
                    recv_sem=recv_sem.at[k],
                    device_id={"rcv": other},
                    device_id_type=MESH,
                ).start()

        def copy_plane(src, block, other):
            return pltpu.make_async_remote_copy(
                src_ref=src,
                dst_ref=nodes_r.at[block],
                send_sem=send_sem.at[0],
                recv_sem=plane_sem.at[block],
                device_id={"rcv": other},
                device_id_type=MESH,
            )

        def wait_plane(block):
            pltpu.make_async_copy(node_blk, nodes_r.at[block], plane_sem.at[block]).wait()

        def wait_for(sem, buf, n, k):
            part = buf.at[pl.ds(0, n - 1)]
            pltpu.make_async_copy(part, part, sem.at[k]).wait()

        loads[0].wait()
        own = pack_blocks(nodes_ref[...].astype(F32))
        node_blk[...] = own[0]
        nodes_r[me_r] = own[0]
        nodes_s[me_s] = own[0]

        def prepare():
            loads[1].wait()
            loads[2].wait()
            loads[3].wait()
            count = count_ref[...]
            live_row = lax.broadcasted_iota(jnp.int32, (1, n_edges), 1) < count
            send_idx = jnp.where(live_row, send_ref[...], -1)
            recv_idx = jnp.where(live_row, recv_ref[...], -1)

            def picker(idx, rows):
                rows_iota = lax.broadcasted_iota(jnp.int32, (rows, n_edges), 0)
                return jnp.where(rows_iota == idx, 1.0, 0.0).astype(F32)

            one_hot_s = picker(send_idx, n_rcv * 8)
            one_hot_r = picker(recv_idx, n_snd * 8)
            take_s[...] = one_hot_s.T.astype(BF16)
            take_r[...] = one_hot_r.T.astype(BF16)
            put_s[...] = one_hot_s.astype(BF16)
            put_r[...] = one_hot_r.astype(BF16)
            loads[4].wait()
            loads[5].wait()
            pre[...] = dot(edges[...], w1[:d])

        late = (me_r - 9) * (me_r - 10) * (me_r - 11) == 0
        pl.when(jnp.logical_not(late))(prepare)

        pl.semaphore_wait(barrier, n_snd - 1 + len(near))
        for step in near:
            copy_plane(node_blk, me_r, plane(step)).start()
        send_snd(lambda o: node_blk, nodes_s, 1)
        pl.when(late)(prepare)
        for step in (-1, 1, -2, 2, -3, 3, -4, 4):
            block = plane(step)
            wait_plane(block)
            if step < 4:
                copy_plane(nodes_r.at[block], block, plane(4 if step < 0 else -4)).start()

        wait_for(recv_sem, nodes_s, n_snd, 1)
        receiver = dot(take_r[...], unpack_blocks(nodes_s[...]).astype(BF16)).astype(BF16)
        pre[...] += dot(receiver, w1[2 * d :])
        for step in (-5, 5, -6, 6, -7, 7, -8):
            wait_plane(plane(step))
        sender = dot(take_s[...], unpack_blocks(nodes_r[...]).astype(BF16)).astype(BF16)
        work[...] = dot(sender, w1[d : 2 * d])
        for start in range(0, n_edges, CHUNK):
            rows = pl.ds(start, CHUNK)
            act = pre[rows] + work[rows]
            pre[rows] = act
            hid[rows] = (act * jax.nn.sigmoid(act)).astype(BF16)
        loads[6].wait()
        work[...] = dot(hid[...], w2[...])
        for start in range(0, n_edges, CHUNK):
            rows = pl.ds(start, CHUNK)
            out, scale = layer_norm(work[rows])
            normed[rows] = out
            inv[rows] = scale
            hid[rows] = out.astype(BF16)
        agg_out[...] = pack_blocks(dot(put_r[...], hid[...]))
        send_snd(lambda o: agg_out.at[o], agg_in, 2)
        agg_in[me_s] = agg_out[me_s]

        loads[7].wait()
        loads[8].wait()
        loads[9].wait()
        loads[10].wait()
        node_pre = dot(nodes_ref[...], nw1[:d])
        for start in range(0, n_edges, CHUNK):
            rows = pl.ds(start, CHUNK)
            act = pre[rows]
            sigma = jax.nn.sigmoid(act)
            slope[rows] = sigma * (1.0 + act * (1.0 - sigma))

        wait_for(recv_sem, agg_in, n_snd, 2)
        aggregate = unpack_sum(agg_in[...]).astype(BF16)
        node_pre = node_pre + dot(aggregate, nw1[d:])
        sigma = jax.nn.sigmoid(node_pre)
        node_out = dot((node_pre * sigma).astype(BF16), nw2[...])
        node_normed, node_inv = layer_norm(node_out)
        gno = gno_ref[...].astype(F32)
        node_gout = norm_backward(gno, node_normed, node_inv).astype(BF16)
        node_gpre = (
            dot_t(node_gout, nw2[...]) * (sigma * (1.0 + node_pre * (1.0 - sigma)))
        ).astype(BF16)
        gagg = pack_blocks(dot_t(node_gpre, nw1[d:]))
        gagg_blk[...] = gagg[0]
        gagg_in[me_s] = gagg[0]
        send_snd(lambda o: gagg_blk, gagg_in, 3)
        direct = gno + dot_t(node_gpre, nw1[:d])

        wait_for(recv_sem, gagg_in, n_snd, 3)
        work[...] = dot(take_r[...], unpack_blocks(gagg_in[...]).astype(BF16))
        for start in range(0, n_edges, CHUNK):
            rows = pl.ds(start, CHUNK)
            live = (
                lax.broadcasted_iota(jnp.int32, (CHUNK, 1), 0) + start < count_ref[...]
            )
            up = work[rows] + jnp.where(live, geo[rows].astype(F32), 0.0)
            hid[rows] = norm_backward(up, normed[rows], inv[rows]).astype(BF16)
        work[...] = dot_t(hid[...], w2[...])
        for start in range(0, n_edges, CHUNK):
            rows = pl.ds(start, CHUNK)
            hid[rows] = (work[rows] * slope[rows]).astype(BF16)
        send_part = dot_t(hid[...], w1[d : 2 * d]).astype(BF16)
        rs_out[...] = pack_blocks(dot(put_s[...], send_part))
        send_rcv(lambda o: rs_out.at[o], rs_in, 4)
        rs_in[me_r] = rs_out[me_r]
        recv_part = dot_t(hid[...], w1[2 * d :]).astype(BF16)
        rr_out[...] = pack_blocks(dot(put_r[...], recv_part))
        send_snd(lambda o: rr_out.at[o], rr_in, 5)
        rr_in[me_s] = rr_out[me_s]
        live_col = lax.broadcasted_iota(jnp.int32, (n_edges, 1), 0) < count_ref[...]
        gedges_ref[...] = jnp.where(live_col, geo[...].astype(F32), 0.0) + dot_t(
            hid[...], w1[:d]
        )

        wait_for(recv_sem, rr_in, n_snd, 5)
        direct = direct + unpack_sum(rr_in[...])
        wait_for(recv_sem, rs_in, n_rcv, 4)
        gnodes_ref[...] = direct + unpack_sum(rs_in[...])

        wait_for(send_sem, nodes_r, n_rcv, 0)
        wait_for(send_sem, nodes_s, n_snd, 1)
        wait_for(send_sem, agg_in, n_snd, 2)
        wait_for(send_sem, gagg_in, n_snd, 3)
        wait_for(send_sem, rs_in, n_rcv, 4)
        wait_for(send_sem, rr_in, n_snd, 5)

    return kernel


def solution(mesh):
    n_snd, n_rcv = mesh.shape["snd"], mesh.shape["rcv"]

    def local(
        nodes,
        edges,
        send_local,
        recv_local,
        edge_count,
        edge_w1,
        edge_w2,
        node_w1,
        node_w2,
        grad_nodes_out,
        grad_edges_out,
    ):
        n_edges, d = edges.shape[2:]
        vmem = pl.BlockSpec(memory_space=pltpu.VMEM)
        hbm = pl.BlockSpec(memory_space=pltpu.HBM)
        half = d // 2
        grad_nodes, grad_edges = pl.pallas_call(
            make_kernel(n_snd, n_rcv),
            out_shape=(
                jax.ShapeDtypeStruct(nodes.shape, F32),
                jax.ShapeDtypeStruct((n_edges, d), F32),
            ),
            in_specs=[hbm] * 11,
            out_specs=(vmem, vmem),
            scratch_shapes=[
                pltpu.VMEM((1, 1), jnp.int32),
                pltpu.VMEM((1, n_edges), jnp.int32),
                pltpu.VMEM((1, n_edges), jnp.int32),
                pltpu.VMEM(nodes.shape, BF16),
                pltpu.VMEM(nodes.shape, BF16),
                pltpu.VMEM((n_edges, d), BF16),
                pltpu.VMEM((n_edges, d), BF16),
                pltpu.VMEM(edge_w1.shape, BF16),
                pltpu.VMEM(edge_w2.shape, BF16),
                pltpu.VMEM(node_w1.shape, BF16),
                pltpu.VMEM(node_w2.shape, BF16),
                pltpu.VMEM((16, half), BF16),
                pltpu.VMEM((n_rcv, 16, half), BF16),
                pltpu.VMEM((n_snd, 16, half), BF16),
                pltpu.VMEM((n_snd, 16, half), BF16),
                pltpu.VMEM((n_snd, 16, half), BF16),
                pltpu.VMEM((16, half), BF16),
                pltpu.VMEM((n_snd, 16, half), BF16),
                pltpu.VMEM((n_rcv, 16, half), BF16),
                pltpu.VMEM((n_rcv, 16, half), BF16),
                pltpu.VMEM((n_snd, 16, half), BF16),
                pltpu.VMEM((n_snd, 16, half), BF16),
                pltpu.VMEM((n_edges, d), F32),
                pltpu.VMEM((n_edges, d), F32),
                pltpu.VMEM((n_edges, 1), F32),
                pltpu.VMEM((n_edges, d), F32),
                pltpu.VMEM((n_edges, d), BF16),
                pltpu.VMEM((n_edges, d), F32),
                pltpu.VMEM((n_rcv * 8, n_edges), BF16),
                pltpu.VMEM((n_snd * 8, n_edges), BF16),
                pltpu.VMEM((n_edges, n_rcv * 8), BF16),
                pltpu.VMEM((n_edges, n_snd * 8), BF16),
                pltpu.SemaphoreType.DMA((11,)),
                pltpu.SemaphoreType.DMA((6,)),
                pltpu.SemaphoreType.DMA((6,)),
                pltpu.SemaphoreType.DMA((n_rcv,)),
            ],
            compiler_params=pltpu.CompilerParams(
                collective_id=0, has_side_effects=True, vmem_limit_bytes=60 * 1024 * 1024
            ),
        )(
            edge_count,
            send_local.reshape(1, n_edges),
            recv_local.reshape(1, n_edges),
            nodes,
            grad_nodes_out,
            edges.reshape(n_edges, d),
            grad_edges_out.reshape(n_edges, d),
            edge_w1,
            edge_w2,
            node_w1,
            node_w2,
        )
        return grad_nodes, grad_edges.reshape(1, 1, n_edges, d)

    in_specs = (
        P(("snd", "rcv"), None),
        P("snd", "rcv", None, None),
        P("snd", "rcv", None),
        P("snd", "rcv", None),
        P("snd", "rcv"),
        P(),
        P(),
        P(),
        P(),
        P(("snd", "rcv"), None),
        P("snd", "rcv", None, None),
    )
    out_specs = (P(("snd", "rcv"), None), P("snd", "rcv", None, None))
    return jax.shard_map(local, mesh=mesh, in_specs=in_specs, out_specs=out_specs, check_vma=False)
```

```python
import itertools

import jax
import jax.numpy as jnp
from jax import lax
from jax.experimental import pallas as pl
from jax.experimental.pallas import tpu as pltpu
from jax.sharding import PartitionSpec as P

MESH = pl.DeviceIdType.MESH
F32 = jnp.float32
BF16 = jnp.bfloat16
CHUNK = 64


def dot(a, b):
    return jnp.dot(a, b, preferred_element_type=F32)


def dot_t(a, b):
    return lax.dot_general(a, b, (((1,), (1,)), ((), ())), preferred_element_type=F32)


def pack_blocks(rows):
    count, width = rows.shape[0] // 8, rows.shape[1]
    blocks = rows.reshape(count, 8, width)
    return jnp.concatenate(
        [blocks[:, :, : width // 2], blocks[:, :, width // 2 :]], axis=1
    ).astype(BF16)


def unpack_blocks(blocks):
    blocks = blocks.astype(F32)
    count, _, half = blocks.shape
    return jnp.concatenate(
        [blocks[:, :8, :].reshape(count * 8, half), blocks[:, 8:, :].reshape(count * 8, half)],
        axis=1,
    )


def unpack_sum(blocks):
    total = jnp.sum(blocks.astype(F32), axis=0)
    return jnp.concatenate([total[:8], total[8:]], axis=1)


def layer_norm(values):
    center = values - jnp.mean(values, -1, keepdims=True)
    inv_scale = lax.rsqrt(jnp.mean(center * center, -1, keepdims=True) + 1e-05)
    return center * inv_scale, inv_scale


def norm_backward(upstream, normed, inv_scale):
    return inv_scale * (
        upstream
        - jnp.mean(upstream, -1, keepdims=True)
        - normed * jnp.mean(upstream * normed, -1, keepdims=True)
    )


def hand_over(grad_nodes, grad_edges):
    def kernel(nodes_in, edges_in, nodes_out, edges_out, sems):
        copies = [
            pltpu.make_async_copy(edges_in, edges_out, sems.at[0]),
            pltpu.make_async_copy(nodes_in, nodes_out, sems.at[1]),
        ]
        for copy in copies:
            copy.start()
        for copy in copies:
            copy.wait()

    vmem = pl.BlockSpec(memory_space=pltpu.VMEM)
    hbm = pl.BlockSpec(memory_space=pltpu.HBM)
    return pl.pallas_call(
        kernel,
        out_shape=(
            jax.ShapeDtypeStruct(grad_nodes.shape, F32),
            jax.ShapeDtypeStruct(grad_edges.shape, F32),
        ),
        in_specs=[vmem, vmem],
        out_specs=(hbm, hbm),
        scratch_shapes=[pltpu.SemaphoreType.DMA((2,))],
    )(
        pltpu.with_memory_space_constraint(grad_nodes, pltpu.VMEM),
        pltpu.with_memory_space_constraint(grad_edges, pltpu.VMEM),
    )


def make_kernel(n_snd, n_rcv):
    far_first = sorted(range(1, n_rcv), key=lambda step: -min(step, n_rcv - step))

    def kernel(
        count_hbm,
        send_hbm,
        recv_hbm,
        nodes_hbm,
        gno_hbm,
        edges_hbm,
        geo_hbm,
        w1_hbm,
        w2_hbm,
        nw1_hbm,
        nw2_hbm,
        gnodes_ref,
        gedges_ref,
        count_ref,
        send_ref,
        recv_ref,
        nodes_ref,
        gno_ref,
        edges,
        geo,
        w1,
        w2,
        nw1,
        nw2,
        node_blk,
        nodes_r,
        nodes_s,
        agg_out,
        agg_in,
        gagg_blk,
        gagg_in,
        rs_out,
        rs_in,
        rr_out,
        rr_in,
        pre,
        normed,
        inv,
        work,
        hid,
        slope,
        put_s,
        put_r,
        take_s,
        take_r,
        load_sem,
        send_sem,
        recv_sem,
        plane_sem,
    ):
        me_s = lax.axis_index("snd")
        me_r = lax.axis_index("rcv")
        n_edges = edges.shape[0]
        d = edges.shape[1]

        loads = [
            pltpu.make_async_copy(src, dst, load_sem.at[k])
            for k, (src, dst) in enumerate(
                [
                    (nodes_hbm, nodes_ref),
                    (count_hbm, count_ref),
                    (send_hbm, send_ref),
                    (recv_hbm, recv_ref),
                    (edges_hbm, edges),
                    (w1_hbm, w1),
                    (w2_hbm, w2),
                    (nw1_hbm, nw1),
                    (nw2_hbm, nw2),
                    (geo_hbm, geo),
                    (gno_hbm, gno_ref),
                ]
            )
        ]
        loads[0].start()

        barrier = pltpu.get_barrier_semaphore()

        def plane(step):
            return (me_r + step + n_rcv) % n_rcv

        cores = [me_s % 2, (me_s + 1) % 2]
        columns = [(me_s // 2 + dx) % 4 * 2 for dx in range(4)]
        lines = [(me_s // 8 + dy) % 4 * 8 for dy in range(4)]
        snd_partners = [
            lines[dy] + columns[dx] + cores[core]
            for dy, dx, core in sorted(
                itertools.product(range(4), range(4), range(2)),
                key=lambda step: -min(step[0], 4 - step[0]) - min(step[1], 4 - step[1]) - step[2] / 2,
            )[:-1]
        ]

        near = (4, -4, 3, -3, 2, -2, 1, -1)
        for step in near:
            pl.semaphore_signal(
                barrier, inc=1, device_id={"rcv": plane(step)}, device_id_type=MESH
            )
        for other in snd_partners:
            pl.semaphore_signal(barrier, inc=1, device_id={"snd": other}, device_id_type=MESH)
        for load in loads[1:]:
            load.start()

        def copy_snd(other, src, dst, k):
            return pltpu.make_async_remote_copy(
                src_ref=src,
                dst_ref=dst.at[me_s],
                send_sem=send_sem.at[k],
                recv_sem=recv_sem.at[k],
                device_id={"snd": other},
                device_id_type=MESH,
            )

        def send_snd(src_of, dst, k):
            for other in snd_partners:
                copy_snd(other, src_of(other), dst, k).start()

        def send_rcv(src_of, dst, k):
            for step in far_first:
                other = (me_r + step) % n_rcv
                pltpu.make_async_remote_copy(
                    src_ref=src_of(other),
                    dst_ref=dst.at[me_r],
                    send_sem=send_sem.at[k],
                    recv_sem=recv_sem.at[k],
                    device_id={"rcv": other},
                    device_id_type=MESH,
                ).start()

        def copy_plane(src, block, other):
            return pltpu.make_async_remote_copy(
                src_ref=src,
                dst_ref=nodes_r.at[block],
                send_sem=send_sem.at[0],
                recv_sem=plane_sem.at[block],
                device_id={"rcv": other},
                device_id_type=MESH,
            )

        def wait_plane(block):
            pltpu.make_async_copy(node_blk, nodes_r.at[block], plane_sem.at[block]).wait()

        def wait_for(sem, buf, n, k):
            part = buf.at[pl.ds(0, n - 1)]
            pltpu.make_async_copy(part, part, sem.at[k]).wait()

        loads[0].wait()
        own = pack_blocks(nodes_ref[...].astype(F32))
        node_blk[...] = own[0]
        nodes_r[me_r] = own[0]
        nodes_s[me_s] = own[0]

        def prepare():
            loads[1].wait()
            loads[2].wait()
            loads[3].wait()
            count = count_ref[...]
            live_row = lax.broadcasted_iota(jnp.int32, (1, n_edges), 1) < count
            send_idx = jnp.where(live_row, send_ref[...], -1)
            recv_idx = jnp.where(live_row, recv_ref[...], -1)

            def picker(idx, rows):
                rows_iota = lax.broadcasted_iota(jnp.int32, (rows, n_edges), 0)
                return jnp.where(rows_iota == idx, 1.0, 0.0).astype(F32)

            one_hot_s = picker(send_idx, n_rcv * 8)
            one_hot_r = picker(recv_idx, n_snd * 8)
            take_s[...] = one_hot_s.T.astype(BF16)
            take_r[...] = one_hot_r.T.astype(BF16)
            put_s[...] = one_hot_s.astype(BF16)
            put_r[...] = one_hot_r.astype(BF16)
            loads[4].wait()
            loads[5].wait()
            pre[...] = dot(edges[...], w1[:d])

        late = me_r >= n_rcv // 2
        pl.when(jnp.logical_not(late))(prepare)

        pl.semaphore_wait(barrier, n_snd - 1 + len(near))
        for step in near:
            copy_plane(node_blk, me_r, plane(step)).start()
        send_snd(lambda o: node_blk, nodes_s, 1)
        pl.when(late)(prepare)
        for step in (-1, 1, -2, 2, -3, 3, -4, 4):
            block = plane(step)
            wait_plane(block)
            if step < 4:
                copy_plane(nodes_r.at[block], block, plane(4 if step < 0 else -4)).start()

        wait_for(recv_sem, nodes_s, n_snd, 1)
        receiver = dot(take_r[...], unpack_blocks(nodes_s[...]).astype(BF16)).astype(BF16)
        pre[...] += dot(receiver, w1[2 * d :])
        for step in (-5, 5, -6, 6, -7, 7, -8):
            wait_plane(plane(step))
        sender = dot(take_s[...], unpack_blocks(nodes_r[...]).astype(BF16)).astype(BF16)
        work[...] = dot(sender, w1[d : 2 * d])
        for start in range(0, n_edges, CHUNK):
            rows = pl.ds(start, CHUNK)
            act = pre[rows] + work[rows]
            pre[rows] = act
            hid[rows] = (act * jax.nn.sigmoid(act)).astype(BF16)
        loads[6].wait()
        work[...] = dot(hid[...], w2[...])
        for start in range(0, n_edges, CHUNK):
            rows = pl.ds(start, CHUNK)
            out, scale = layer_norm(work[rows])
            normed[rows] = out
            inv[rows] = scale
            hid[rows] = out.astype(BF16)
        agg_out[...] = pack_blocks(dot(put_r[...], hid[...]))
        send_snd(lambda o: agg_out.at[o], agg_in, 2)
        agg_in[me_s] = agg_out[me_s]

        loads[7].wait()
        loads[8].wait()
        loads[9].wait()
        loads[10].wait()
        node_pre = dot(nodes_ref[...], nw1[:d])
        for start in range(0, n_edges, CHUNK):
            rows = pl.ds(start, CHUNK)
            act = pre[rows]
            sigma = jax.nn.sigmoid(act)
            slope[rows] = sigma * (1.0 + act * (1.0 - sigma))

        wait_for(recv_sem, agg_in, n_snd, 2)
        aggregate = unpack_sum(agg_in[...]).astype(BF16)
        node_pre = node_pre + dot(aggregate, nw1[d:])
        sigma = jax.nn.sigmoid(node_pre)
        node_out = dot((node_pre * sigma).astype(BF16), nw2[...])
        node_normed, node_inv = layer_norm(node_out)
        gno = gno_ref[...].astype(F32)
        node_gout = norm_backward(gno, node_normed, node_inv).astype(BF16)
        node_gpre = (
            dot_t(node_gout, nw2[...]) * (sigma * (1.0 + node_pre * (1.0 - sigma)))
        ).astype(BF16)
        gagg = pack_blocks(dot_t(node_gpre, nw1[d:]))
        gagg_blk[...] = gagg[0]
        gagg_in[me_s] = gagg[0]
        send_snd(lambda o: gagg_blk, gagg_in, 3)
        direct = gno + dot_t(node_gpre, nw1[:d])

        wait_for(recv_sem, gagg_in, n_snd, 3)
        work[...] = dot(take_r[...], unpack_blocks(gagg_in[...]).astype(BF16))
        for start in range(0, n_edges, CHUNK):
            rows = pl.ds(start, CHUNK)
            live = (
                lax.broadcasted_iota(jnp.int32, (CHUNK, 1), 0) + start < count_ref[...]
            )
            up = work[rows] + jnp.where(live, geo[rows].astype(F32), 0.0)
            hid[rows] = norm_backward(up, normed[rows], inv[rows]).astype(BF16)
        work[...] = dot_t(hid[...], w2[...])
        for start in range(0, n_edges, CHUNK):
            rows = pl.ds(start, CHUNK)
            hid[rows] = (work[rows] * slope[rows]).astype(BF16)
        send_part = dot_t(hid[...], w1[d : 2 * d]).astype(BF16)
        rs_out[...] = pack_blocks(dot(put_s[...], send_part))
        send_rcv(lambda o: rs_out.at[o], rs_in, 4)
        rs_in[me_r] = rs_out[me_r]
        recv_part = dot_t(hid[...], w1[2 * d :]).astype(BF16)
        rr_out[...] = pack_blocks(dot(put_r[...], recv_part))
        send_snd(lambda o: rr_out.at[o], rr_in, 5)
        rr_in[me_s] = rr_out[me_s]
        live_col = lax.broadcasted_iota(jnp.int32, (n_edges, 1), 0) < count_ref[...]
        gedges_ref[...] = jnp.where(live_col, geo[...].astype(F32), 0.0) + dot_t(
            hid[...], w1[:d]
        )

        wait_for(recv_sem, rr_in, n_snd, 5)
        direct = direct + unpack_sum(rr_in[...])
        wait_for(recv_sem, rs_in, n_rcv, 4)
        gnodes_ref[...] = direct + unpack_sum(rs_in[...])

        wait_for(send_sem, nodes_r, n_rcv, 0)
        wait_for(send_sem, nodes_s, n_snd, 1)
        wait_for(send_sem, agg_in, n_snd, 2)
        wait_for(send_sem, gagg_in, n_snd, 3)
        wait_for(send_sem, rs_in, n_rcv, 4)
        wait_for(send_sem, rr_in, n_snd, 5)

    return kernel


def solution(mesh):
    n_snd, n_rcv = mesh.shape["snd"], mesh.shape["rcv"]

    def local(
        nodes,
        edges,
        send_local,
        recv_local,
        edge_count,
        edge_w1,
        edge_w2,
        node_w1,
        node_w2,
        grad_nodes_out,
        grad_edges_out,
    ):
        n_edges, d = edges.shape[2:]
        vmem = pl.BlockSpec(memory_space=pltpu.VMEM)
        hbm = pl.BlockSpec(memory_space=pltpu.HBM)
        half = d // 2
        grad_nodes, grad_edges = pl.pallas_call(
            make_kernel(n_snd, n_rcv),
            out_shape=(
                pltpu.VMEM(nodes.shape, F32),
                pltpu.VMEM((n_edges, d), F32),
            ),
            in_specs=[hbm] * 11,
            out_specs=(vmem, vmem),
            scratch_shapes=[
                pltpu.VMEM((1, 1), jnp.int32),
                pltpu.VMEM((1, n_edges), jnp.int32),
                pltpu.VMEM((1, n_edges), jnp.int32),
                pltpu.VMEM(nodes.shape, BF16),
                pltpu.VMEM(nodes.shape, BF16),
                pltpu.VMEM((n_edges, d), BF16),
                pltpu.VMEM((n_edges, d), BF16),
                pltpu.VMEM(edge_w1.shape, BF16),
                pltpu.VMEM(edge_w2.shape, BF16),
                pltpu.VMEM(node_w1.shape, BF16),
                pltpu.VMEM(node_w2.shape, BF16),
                pltpu.VMEM((16, half), BF16),
                pltpu.VMEM((n_rcv, 16, half), BF16),
                pltpu.VMEM((n_snd, 16, half), BF16),
                pltpu.VMEM((n_snd, 16, half), BF16),
                pltpu.VMEM((n_snd, 16, half), BF16),
                pltpu.VMEM((16, half), BF16),
                pltpu.VMEM((n_snd, 16, half), BF16),
                pltpu.VMEM((n_rcv, 16, half), BF16),
                pltpu.VMEM((n_rcv, 16, half), BF16),
                pltpu.VMEM((n_snd, 16, half), BF16),
                pltpu.VMEM((n_snd, 16, half), BF16),
                pltpu.VMEM((n_edges, d), F32),
                pltpu.VMEM((n_edges, d), F32),
                pltpu.VMEM((n_edges, 1), F32),
                pltpu.VMEM((n_edges, d), F32),
                pltpu.VMEM((n_edges, d), BF16),
                pltpu.VMEM((n_edges, d), F32),
                pltpu.VMEM((n_rcv * 8, n_edges), BF16),
                pltpu.VMEM((n_snd * 8, n_edges), BF16),
                pltpu.VMEM((n_edges, n_rcv * 8), BF16),
                pltpu.VMEM((n_edges, n_snd * 8), BF16),
                pltpu.SemaphoreType.DMA((11,)),
                pltpu.SemaphoreType.DMA((6,)),
                pltpu.SemaphoreType.DMA((6,)),
                pltpu.SemaphoreType.DMA((n_rcv,)),
            ],
            compiler_params=pltpu.CompilerParams(
                collective_id=0, has_side_effects=True, vmem_limit_bytes=48 * 1024 * 1024
            ),
        )(
            edge_count,
            *(
                pltpu.with_memory_space_constraint(operand, pltpu.HBM)
                for operand in (
                    send_local.reshape(1, n_edges),
                    recv_local.reshape(1, n_edges),
                    nodes,
                    grad_nodes_out,
                    edges.reshape(n_edges, d),
                    grad_edges_out.reshape(n_edges, d),
                    edge_w1,
                    edge_w2,
                    node_w1,
                    node_w2,
                )
            )
        )
        grad_nodes, grad_edges = hand_over(grad_nodes, grad_edges)
        return grad_nodes, grad_edges.reshape(1, 1, n_edges, d)

    in_specs = (
        P(("snd", "rcv"), None),
        P("snd", "rcv", None, None),
        P("snd", "rcv", None),
        P("snd", "rcv", None),
        P("snd", "rcv"),
        P(),
        P(),
        P(),
        P(),
        P(("snd", "rcv"), None),
        P("snd", "rcv", None, None),
    )
    out_specs = (P(("snd", "rcv"), None), P("snd", "rcv", None, None))
    return jax.shard_map(local, mesh=mesh, in_specs=in_specs, out_specs=out_specs, check_vma=False)
```

```python
import itertools

import jax
import jax.numpy as jnp
from jax import lax
from jax.experimental import pallas as pl
from jax.experimental.pallas import tpu as pltpu
from jax.sharding import PartitionSpec as P

MESH = pl.DeviceIdType.MESH
F32 = jnp.float32
BF16 = jnp.bfloat16
CHUNK = 64


def dot(a, b):
    return jnp.dot(a, b, preferred_element_type=F32)


def dot_t(a, b):
    return lax.dot_general(a, b, (((1,), (1,)), ((), ())), preferred_element_type=F32)


def pack_blocks(rows):
    count, width = rows.shape[0] // 8, rows.shape[1]
    blocks = rows.reshape(count, 8, width)
    return jnp.concatenate(
        [blocks[:, :, : width // 2], blocks[:, :, width // 2 :]], axis=1
    ).astype(BF16)


def unpack_blocks(blocks):
    blocks = blocks.astype(F32)
    count, _, half = blocks.shape
    return jnp.concatenate(
        [blocks[:, :8, :].reshape(count * 8, half), blocks[:, 8:, :].reshape(count * 8, half)],
        axis=1,
    )


def unpack_sum(blocks):
    total = jnp.sum(blocks.astype(F32), axis=0)
    return jnp.concatenate([total[:8], total[8:]], axis=1)


def layer_norm(values):
    center = values - jnp.mean(values, -1, keepdims=True)
    inv_scale = lax.rsqrt(jnp.mean(center * center, -1, keepdims=True) + 1e-05)
    return center * inv_scale, inv_scale


def norm_backward(upstream, normed, inv_scale):
    return inv_scale * (
        upstream
        - jnp.mean(upstream, -1, keepdims=True)
        - normed * jnp.mean(upstream * normed, -1, keepdims=True)
    )


def hand_over(grad_nodes, grad_edges):
    def kernel(nodes_in, edges_in, nodes_out, edges_out, sems):
        copies = [
            pltpu.make_async_copy(edges_in, edges_out, sems.at[0]),
            pltpu.make_async_copy(nodes_in, nodes_out, sems.at[1]),
        ]
        for copy in copies:
            copy.start()
        for copy in copies:
            copy.wait()

    vmem = pl.BlockSpec(memory_space=pltpu.VMEM)
    hbm = pl.BlockSpec(memory_space=pltpu.HBM)
    return pl.pallas_call(
        kernel,
        out_shape=(
            jax.ShapeDtypeStruct(grad_nodes.shape, F32),
            jax.ShapeDtypeStruct(grad_edges.shape, F32),
        ),
        in_specs=[vmem, vmem],
        out_specs=(hbm, hbm),
        scratch_shapes=[pltpu.SemaphoreType.DMA((2,))],
    )(
        pltpu.with_memory_space_constraint(grad_nodes, pltpu.VMEM),
        pltpu.with_memory_space_constraint(grad_edges, pltpu.VMEM),
    )


def make_kernel(n_snd, n_rcv):
    far_first = sorted(range(1, n_rcv), key=lambda step: -min(step, n_rcv - step))

    def kernel(
        count_hbm,
        send_hbm,
        recv_hbm,
        nodes_hbm,
        gno_hbm,
        edges_hbm,
        geo_hbm,
        w1_hbm,
        w2_hbm,
        nw1_hbm,
        nw2_hbm,
        gnodes_ref,
        gedges_ref,
        count_ref,
        send_ref,
        recv_ref,
        nodes_ref,
        gno_ref,
        edges,
        geo,
        w1,
        w2,
        nw1,
        nw2,
        node_blk,
        nodes_r,
        nodes_s,
        agg_out,
        agg_in,
        gagg_blk,
        gagg_in,
        rs_out,
        rs_in,
        rr_out,
        rr_in,
        pre,
        normed,
        inv,
        work,
        hid,
        slope,
        put_s,
        put_r,
        take_s,
        take_r,
        load_sem,
        send_sem,
        recv_sem,
        plane_sem,
    ):
        me_s = lax.axis_index("snd")
        me_r = lax.axis_index("rcv")
        n_edges = edges.shape[0]
        d = edges.shape[1]

        loads = [
            pltpu.make_async_copy(src, dst, load_sem.at[k])
            for k, (src, dst) in enumerate(
                [
                    (nodes_hbm, nodes_ref),
                    (count_hbm, count_ref),
                    (send_hbm, send_ref),
                    (recv_hbm, recv_ref),
                    (edges_hbm, edges),
                    (w1_hbm, w1),
                    (w2_hbm, w2),
                    (nw1_hbm, nw1),
                    (nw2_hbm, nw2),
                    (geo_hbm, geo),
                    (gno_hbm, gno_ref),
                ]
            )
        ]
        loads[0].start()

        barrier = pltpu.get_barrier_semaphore()

        def plane(step):
            return (me_r + step + n_rcv) % n_rcv

        cores = [me_s % 2, (me_s + 1) % 2]
        columns = [(me_s // 2 + dx) % 4 * 2 for dx in range(4)]
        lines = [(me_s // 8 + dy) % 4 * 8 for dy in range(4)]
        chips = sorted(
            itertools.product(range(4), range(4)),
            key=lambda step: -min(step[0], 4 - step[0]) - min(step[1], 4 - step[1]),
        )
        same_core, other_core = (
            [lines[dy] + columns[dx] + cores[core] for dy, dx in chips] for core in range(2)
        )
        same_core, sibling = same_core[:-1], other_core[-1]
        snd_partners = other_core + same_core

        near = (4, -4, 3, -3, 2, -2, 1, -1)
        for step in near:
            pl.semaphore_signal(
                barrier, inc=1, device_id={"rcv": plane(step)}, device_id_type=MESH
            )
        for other in same_core + [sibling]:
            pl.semaphore_signal(barrier, inc=1, device_id={"snd": other}, device_id_type=MESH)
        for load in loads[1:]:
            load.start()

        def copy_snd(other, src, dst, k):
            return pltpu.make_async_remote_copy(
                src_ref=src,
                dst_ref=dst.at[me_s],
                send_sem=send_sem.at[k],
                recv_sem=recv_sem.at[k],
                device_id={"snd": other},
                device_id_type=MESH,
            )

        def copy_sibling(src, block):
            return pltpu.make_async_remote_copy(
                src_ref=src,
                dst_ref=nodes_s.at[block],
                send_sem=send_sem.at[1],
                recv_sem=recv_sem.at[0],
                device_id={"snd": sibling},
                device_id_type=MESH,
            )

        def send_snd(src_of, dst, k):
            for other in snd_partners:
                copy_snd(other, src_of(other), dst, k).start()

        def send_rcv(src_of, dst, k):
            for rank in range(n_rcv - 1):
                other = rank + jnp.where(rank >= me_r, 1, 0)
                pltpu.make_async_remote_copy(
                    src_ref=src_of(other),
                    dst_ref=dst.at[me_r],
                    send_sem=send_sem.at[k],
                    recv_sem=recv_sem.at[k],
                    device_id={"rcv": other},
                    device_id_type=MESH,
                ).start()

        def copy_plane(src, block, other):
            return pltpu.make_async_remote_copy(
                src_ref=src,
                dst_ref=nodes_r.at[block],
                send_sem=send_sem.at[0],
                recv_sem=plane_sem.at[block],
                device_id={"rcv": other},
                device_id_type=MESH,
            )

        def wait_plane(block):
            pltpu.make_async_copy(node_blk, nodes_r.at[block], plane_sem.at[block]).wait()

        def wait_for(sem, buf, n, k):
            part = buf.at[pl.ds(0, n - 1)]
            pltpu.make_async_copy(part, part, sem.at[k]).wait()

        loads[0].wait()
        own = pack_blocks(nodes_ref[...].astype(F32))
        node_blk[...] = own[0]
        nodes_r[me_r] = own[0]
        nodes_s[me_s] = own[0]

        def prepare():
            loads[1].wait()
            loads[2].wait()
            loads[3].wait()
            count = count_ref[...]
            live_row = lax.broadcasted_iota(jnp.int32, (1, n_edges), 1) < count
            send_idx = jnp.where(live_row, send_ref[...], -1)
            recv_idx = jnp.where(live_row, recv_ref[...], -1)

            def picker(idx, rows):
                rows_iota = lax.broadcasted_iota(jnp.int32, (rows, n_edges), 0)
                return jnp.where(rows_iota == idx, 1.0, 0.0).astype(F32)

            one_hot_s = picker(send_idx, n_rcv * 8)
            one_hot_r = picker(recv_idx, n_snd * 8)
            take_s[...] = one_hot_s.T.astype(BF16)
            take_r[...] = one_hot_r.T.astype(BF16)
            put_s[...] = one_hot_s.astype(BF16)
            put_r[...] = one_hot_r.astype(BF16)
            loads[4].wait()
            loads[5].wait()
            pre[...] = dot(edges[...], w1[:d])

        late = me_r >= n_rcv // 2
        pl.when(jnp.logical_not(late))(prepare)

        pl.semaphore_wait(barrier, len(near) + len(same_core) + 1)
        for step in near:
            copy_plane(node_blk, me_r, plane(step)).start()
        for other in same_core:
            copy_snd(other, node_blk, nodes_s, 1).start()
        copy_sibling(node_blk, me_s).start()
        pl.when(late)(prepare)
        for step in (-1, 1, -2, 2, -3, 3, -4, 4):
            block = plane(step)
            wait_plane(block)
            if step < 4:
                copy_plane(nodes_r.at[block], block, plane(4 if step < 0 else -4)).start()

        wait_for(recv_sem, nodes_s, n_snd // 2, 1)
        for block in same_core:
            copy_sibling(nodes_s.at[block], block).start()
        wait_for(recv_sem, nodes_s, n_snd // 2 + 1, 0)
        receiver = dot(take_r[...], unpack_blocks(nodes_s[...]).astype(BF16)).astype(BF16)
        pre[...] += dot(receiver, w1[2 * d :])
        for step in (-5, 5, -6, 6, -7, 7, -8):
            wait_plane(plane(step))
        sender = dot(take_s[...], unpack_blocks(nodes_r[...]).astype(BF16)).astype(BF16)
        work[...] = dot(sender, w1[d : 2 * d])
        for start in range(0, n_edges, CHUNK):
            rows = pl.ds(start, CHUNK)
            act = pre[rows] + work[rows]
            pre[rows] = act
            hid[rows] = (act * jax.nn.sigmoid(act)).astype(BF16)
        loads[6].wait()
        work[...] = dot(hid[...], w2[...])
        for start in range(0, n_edges, CHUNK):
            rows = pl.ds(start, CHUNK)
            out, scale = layer_norm(work[rows])
            normed[rows] = out
            inv[rows] = scale
            hid[rows] = out.astype(BF16)
        agg_out[...] = pack_blocks(dot(put_r[...], hid[...]))
        send_snd(lambda o: agg_out.at[o], agg_in, 2)
        agg_in[me_s] = agg_out[me_s]

        loads[7].wait()
        loads[8].wait()
        loads[9].wait()
        loads[10].wait()
        node_pre = dot(nodes_ref[...], nw1[:d])
        for start in range(0, n_edges, CHUNK):
            rows = pl.ds(start, CHUNK)
            act = pre[rows]
            sigma = jax.nn.sigmoid(act)
            slope[rows] = sigma * (1.0 + act * (1.0 - sigma))

        wait_for(recv_sem, agg_in, n_snd, 2)
        aggregate = unpack_sum(agg_in[...]).astype(BF16)
        node_pre = node_pre + dot(aggregate, nw1[d:])
        sigma = jax.nn.sigmoid(node_pre)
        node_out = dot((node_pre * sigma).astype(BF16), nw2[...])
        node_normed, node_inv = layer_norm(node_out)
        gno = gno_ref[...].astype(F32)
        node_gout = norm_backward(gno, node_normed, node_inv).astype(BF16)
        node_gpre = (
            dot_t(node_gout, nw2[...]) * (sigma * (1.0 + node_pre * (1.0 - sigma)))
        ).astype(BF16)
        gagg = pack_blocks(dot_t(node_gpre, nw1[d:]))
        gagg_blk[...] = gagg[0]
        gagg_in[me_s] = gagg[0]
        send_snd(lambda o: gagg_blk, gagg_in, 3)
        direct = gno + dot_t(node_gpre, nw1[:d])

        wait_for(recv_sem, gagg_in, n_snd, 3)
        work[...] = dot(take_r[...], unpack_blocks(gagg_in[...]).astype(BF16))
        for start in range(0, n_edges, CHUNK):
            rows = pl.ds(start, CHUNK)
            live = (
                lax.broadcasted_iota(jnp.int32, (CHUNK, 1), 0) + start < count_ref[...]
            )
            up = work[rows] + jnp.where(live, geo[rows].astype(F32), 0.0)
            hid[rows] = norm_backward(up, normed[rows], inv[rows]).astype(BF16)
        work[...] = dot_t(hid[...], w2[...])
        for start in range(0, n_edges, CHUNK):
            rows = pl.ds(start, CHUNK)
            hid[rows] = (work[rows] * slope[rows]).astype(BF16)
        send_part = dot(put_s[...], hid[...]).astype(BF16)
        rs_out[...] = pack_blocks(dot_t(send_part, w1[d : 2 * d]))
        send_rcv(lambda o: rs_out.at[o], rs_in, 4)
        rs_in[me_r] = rs_out[me_r]
        recv_part = dot_t(hid[...], w1[2 * d :]).astype(BF16)
        rr_out[...] = pack_blocks(dot(put_r[...], recv_part))
        send_snd(lambda o: rr_out.at[o], rr_in, 5)
        rr_in[me_s] = rr_out[me_s]
        live_col = lax.broadcasted_iota(jnp.int32, (n_edges, 1), 0) < count_ref[...]
        gedges_ref[...] = jnp.where(live_col, geo[...].astype(F32), 0.0) + dot_t(
            hid[...], w1[:d]
        )

        wait_for(recv_sem, rr_in, n_snd, 5)
        direct = direct + unpack_sum(rr_in[...])
        wait_for(recv_sem, rs_in, n_rcv, 4)
        gnodes_ref[...] = direct + unpack_sum(rs_in[...])

        wait_for(send_sem, nodes_r, n_rcv, 0)
        wait_for(send_sem, nodes_s, n_snd, 1)
        wait_for(send_sem, agg_in, n_snd, 2)
        wait_for(send_sem, gagg_in, n_snd, 3)
        wait_for(send_sem, rs_in, n_rcv, 4)
        wait_for(send_sem, rr_in, n_snd, 5)

    return kernel


def solution(mesh):
    n_snd, n_rcv = mesh.shape["snd"], mesh.shape["rcv"]

    def local(
        nodes,
        edges,
        send_local,
        recv_local,
        edge_count,
        edge_w1,
        edge_w2,
        node_w1,
        node_w2,
        grad_nodes_out,
        grad_edges_out,
    ):
        n_edges, d = edges.shape[2:]
        vmem = pl.BlockSpec(memory_space=pltpu.VMEM)
        hbm = pl.BlockSpec(memory_space=pltpu.HBM)
        half = d // 2
        grad_nodes, grad_edges = pl.pallas_call(
            make_kernel(n_snd, n_rcv),
            out_shape=(
                pltpu.VMEM(nodes.shape, F32),
                pltpu.VMEM((n_edges, d), F32),
            ),
            in_specs=[hbm] * 11,
            out_specs=(vmem, vmem),
            scratch_shapes=[
                pltpu.VMEM((1, 1), jnp.int32),
                pltpu.VMEM((1, n_edges), jnp.int32),
                pltpu.VMEM((1, n_edges), jnp.int32),
                pltpu.VMEM(nodes.shape, BF16),
                pltpu.VMEM(nodes.shape, BF16),
                pltpu.VMEM((n_edges, d), BF16),
                pltpu.VMEM((n_edges, d), BF16),
                pltpu.VMEM(edge_w1.shape, BF16),
                pltpu.VMEM(edge_w2.shape, BF16),
                pltpu.VMEM(node_w1.shape, BF16),
                pltpu.VMEM(node_w2.shape, BF16),
                pltpu.VMEM((16, half), BF16),
                pltpu.VMEM((n_rcv, 16, half), BF16),
                pltpu.VMEM((n_snd, 16, half), BF16),
                pltpu.VMEM((n_snd, 16, half), BF16),
                pltpu.VMEM((n_snd, 16, half), BF16),
                pltpu.VMEM((16, half), BF16),
                pltpu.VMEM((n_snd, 16, half), BF16),
                pltpu.VMEM((n_rcv, 16, half), BF16),
                pltpu.VMEM((n_rcv, 16, half), BF16),
                pltpu.VMEM((n_snd, 16, half), BF16),
                pltpu.VMEM((n_snd, 16, half), BF16),
                pltpu.VMEM((n_edges, d), F32),
                pltpu.VMEM((n_edges, d), F32),
                pltpu.VMEM((n_edges, 1), F32),
                pltpu.VMEM((n_edges, d), F32),
                pltpu.VMEM((n_edges, d), BF16),
                pltpu.VMEM((n_edges, d), F32),
                pltpu.VMEM((n_rcv * 8, n_edges), BF16),
                pltpu.VMEM((n_snd * 8, n_edges), BF16),
                pltpu.VMEM((n_edges, n_rcv * 8), BF16),
                pltpu.VMEM((n_edges, n_snd * 8), BF16),
                pltpu.SemaphoreType.DMA((11,)),
                pltpu.SemaphoreType.DMA((6,)),
                pltpu.SemaphoreType.DMA((6,)),
                pltpu.SemaphoreType.DMA((n_rcv,)),
            ],
            compiler_params=pltpu.CompilerParams(
                collective_id=0, has_side_effects=True, vmem_limit_bytes=48 * 1024 * 1024
            ),
        )(
            edge_count,
            *(
                pltpu.with_memory_space_constraint(operand, pltpu.HBM)
                for operand in (
                    send_local.reshape(1, n_edges),
                    recv_local.reshape(1, n_edges),
                    nodes,
                    grad_nodes_out,
                    edges.reshape(n_edges, d),
                    grad_edges_out.reshape(n_edges, d),
                    edge_w1,
                    edge_w2,
                    node_w1,
                    node_w2,
                )
            )
        )
        grad_nodes, grad_edges = hand_over(grad_nodes, grad_edges)
        return grad_nodes, grad_edges.reshape(1, 1, n_edges, d)

    in_specs = (
        P(("snd", "rcv"), None),
        P("snd", "rcv", None, None),
        P("snd", "rcv", None),
        P("snd", "rcv", None),
        P("snd", "rcv"),
        P(),
        P(),
        P(),
        P(),
        P(("snd", "rcv"), None),
        P("snd", "rcv", None, None),
    )
    out_specs = (P(("snd", "rcv"), None), P("snd", "rcv", None, None))
    return jax.shard_map(local, mesh=mesh, in_specs=in_specs, out_specs=out_specs, check_vma=False)
```

```python
import itertools

import jax
import jax.numpy as jnp
from jax import lax
from jax.experimental import pallas as pl
from jax.experimental.pallas import tpu as pltpu
from jax.sharding import PartitionSpec as P

MESH = pl.DeviceIdType.MESH
F32 = jnp.float32
BF16 = jnp.bfloat16
CHUNK = 64


def dot(a, b):
    return jnp.dot(a, b, preferred_element_type=F32)


def dot_t(a, b):
    return lax.dot_general(a, b, (((1,), (1,)), ((), ())), preferred_element_type=F32)


def pack_blocks(rows):
    count, width = rows.shape[0] // 8, rows.shape[1]
    blocks = rows.reshape(count, 8, width)
    return jnp.concatenate(
        [blocks[:, :, : width // 2], blocks[:, :, width // 2 :]], axis=1
    ).astype(BF16)


def unpack_blocks(blocks):
    blocks = blocks.astype(F32)
    count, _, half = blocks.shape
    return jnp.concatenate(
        [blocks[:, :8, :].reshape(count * 8, half), blocks[:, 8:, :].reshape(count * 8, half)],
        axis=1,
    )


def unpack_sum(blocks):
    total = jnp.sum(blocks.astype(F32), axis=0)
    return jnp.concatenate([total[:8], total[8:]], axis=1)


def layer_norm(values):
    center = values - jnp.mean(values, -1, keepdims=True)
    inv_scale = lax.rsqrt(jnp.mean(center * center, -1, keepdims=True) + 1e-05)
    return center * inv_scale, inv_scale


def norm_backward(upstream, normed, inv_scale):
    return inv_scale * (
        upstream
        - jnp.mean(upstream, -1, keepdims=True)
        - normed * jnp.mean(upstream * normed, -1, keepdims=True)
    )


def hand_over(grad_nodes, grad_edges):
    def kernel(nodes_in, edges_in, nodes_out, edges_out, sems):
        copies = [
            pltpu.make_async_copy(edges_in, edges_out, sems.at[0]),
            pltpu.make_async_copy(nodes_in, nodes_out, sems.at[1]),
        ]
        for copy in copies:
            copy.start()
        for copy in copies:
            copy.wait()

    vmem = pl.BlockSpec(memory_space=pltpu.VMEM)
    hbm = pl.BlockSpec(memory_space=pltpu.HBM)
    return pl.pallas_call(
        kernel,
        out_shape=(
            jax.ShapeDtypeStruct(grad_nodes.shape, F32),
            jax.ShapeDtypeStruct(grad_edges.shape, F32),
        ),
        in_specs=[vmem, vmem],
        out_specs=(hbm, hbm),
        scratch_shapes=[pltpu.SemaphoreType.DMA((2,))],
    )(
        pltpu.with_memory_space_constraint(grad_nodes, pltpu.VMEM),
        pltpu.with_memory_space_constraint(grad_edges, pltpu.VMEM),
    )


def make_kernel(n_snd, n_rcv):
    far_first = sorted(range(1, n_rcv), key=lambda step: -min(step, n_rcv - step))

    def kernel(
        count_hbm,
        send_hbm,
        recv_hbm,
        nodes_hbm,
        gno_hbm,
        edges_hbm,
        geo_hbm,
        w1_hbm,
        w2_hbm,
        nw1_hbm,
        nw2_hbm,
        gnodes_ref,
        gedges_ref,
        count_ref,
        send_ref,
        recv_ref,
        nodes_ref,
        gno_ref,
        edges,
        geo,
        w1,
        w2,
        nw1,
        nw2,
        node_blk,
        nodes_r,
        nodes_s,
        agg_out,
        agg_in,
        gagg_blk,
        gagg_in,
        rs_out,
        rs_in,
        rr_out,
        rr_in,
        pre,
        normed,
        inv,
        work,
        hid,
        slope,
        put_s,
        put_r,
        take_s,
        take_r,
        load_sem,
        send_sem,
        recv_sem,
        plane_sem,
        turn_sem,
    ):
        me_s = lax.axis_index("snd")
        me_r = lax.axis_index("rcv")
        n_edges = edges.shape[0]
        d = edges.shape[1]

        loads = [
            pltpu.make_async_copy(src, dst, load_sem.at[k])
            for k, (src, dst) in enumerate(
                [
                    (nodes_hbm, nodes_ref),
                    (count_hbm, count_ref),
                    (send_hbm, send_ref),
                    (recv_hbm, recv_ref),
                    (edges_hbm, edges),
                    (w1_hbm, w1),
                    (w2_hbm, w2),
                    (nw1_hbm, nw1),
                    (nw2_hbm, nw2),
                    (geo_hbm, geo),
                    (gno_hbm, gno_ref),
                ]
            )
        ]
        loads[0].start()

        barrier = pltpu.get_barrier_semaphore()

        def plane(step):
            return (me_r + step + n_rcv) % n_rcv

        cores = [me_s % 2, (me_s + 1) % 2]
        columns = [(me_s // 2 + dx) % 4 * 2 for dx in range(4)]
        lines = [(me_s // 8 + dy) % 4 * 8 for dy in range(4)]
        chips = sorted(
            itertools.product(range(4), range(4)),
            key=lambda step: -min(step[0], 4 - step[0]) - min(step[1], 4 - step[1]),
        )
        same_core, other_core = (
            [lines[dy] + columns[dx] + cores[core] for dy, dx in chips] for core in range(2)
        )
        same_core, sibling = same_core[:-1], other_core[-1]
        greeted = same_core[1:]
        two_lines, two_columns = (same_core[chips.index(chip)] for chip in ((2, 0), (0, 2)))
        snd_partners = other_core + same_core

        near = (3, -3, 2, -2, 1, -1)
        passed = ((-2, (2,)), (2, (-2,)), (-3, (5, 4, 3, 2)), (3, (-4, -3, -2)))
        for step in near:
            pl.semaphore_signal(
                barrier, inc=1, device_id={"rcv": plane(step)}, device_id_type=MESH
            )
        for other in greeted + [sibling]:
            pl.semaphore_signal(barrier, inc=1, device_id={"snd": other}, device_id_type=MESH)
        for load in loads[1:]:
            load.start()

        def copy_snd(other, src, dst, k):
            return pltpu.make_async_remote_copy(
                src_ref=src,
                dst_ref=dst.at[me_s],
                send_sem=send_sem.at[k],
                recv_sem=recv_sem.at[k],
                device_id={"snd": other},
                device_id_type=MESH,
            )

        def copy_turn(other, src, block, turn):
            return pltpu.make_async_remote_copy(
                src_ref=src,
                dst_ref=nodes_s.at[block],
                send_sem=send_sem.at[1],
                recv_sem=turn_sem if turn else recv_sem.at[1],
                device_id={"snd": other},
                device_id_type=MESH,
            )

        def copy_sibling(src, block):
            return pltpu.make_async_remote_copy(
                src_ref=src,
                dst_ref=nodes_s.at[block],
                send_sem=send_sem.at[1],
                recv_sem=recv_sem.at[0],
                device_id={"snd": sibling},
                device_id_type=MESH,
            )

        def send_snd(src_of, dst, k):
            for other in snd_partners:
                copy_snd(other, src_of(other), dst, k).start()

        def send_rcv(src_of, dst, k):
            for rank in range(n_rcv - 1):
                other = rank + jnp.where(rank >= me_r, 1, 0)
                pltpu.make_async_remote_copy(
                    src_ref=src_of(other),
                    dst_ref=dst.at[me_r],
                    send_sem=send_sem.at[k],
                    recv_sem=recv_sem.at[k],
                    device_id={"rcv": other},
                    device_id_type=MESH,
                ).start()

        def copy_plane(src, block, other):
            return pltpu.make_async_remote_copy(
                src_ref=src,
                dst_ref=nodes_r.at[block],
                send_sem=send_sem.at[0],
                recv_sem=plane_sem.at[block],
                device_id={"rcv": other},
                device_id_type=MESH,
            )

        def wait_plane(block):
            pltpu.make_async_copy(node_blk, nodes_r.at[block], plane_sem.at[block]).wait()

        def wait_for(sem, buf, n, k):
            part = buf.at[pl.ds(0, n - 1)]
            pltpu.make_async_copy(part, part, sem.at[k]).wait()

        loads[0].wait()
        own = pack_blocks(nodes_ref[...].astype(F32))
        node_blk[...] = own[0]
        nodes_r[me_r] = own[0]
        nodes_s[me_s] = own[0]

        def prepare():
            loads[1].wait()
            loads[2].wait()
            loads[3].wait()
            count = count_ref[...]
            live_row = lax.broadcasted_iota(jnp.int32, (1, n_edges), 1) < count
            send_idx = jnp.where(live_row, send_ref[...], -1)
            recv_idx = jnp.where(live_row, recv_ref[...], -1)

            def picker(idx, rows):
                rows_iota = lax.broadcasted_iota(jnp.int32, (rows, n_edges), 0)
                return jnp.where(rows_iota == idx, 1.0, 0.0).astype(F32)

            one_hot_s = picker(send_idx, n_rcv * 8)
            one_hot_r = picker(recv_idx, n_snd * 8)
            take_s[...] = one_hot_s.T.astype(BF16)
            take_r[...] = one_hot_r.T.astype(BF16)
            put_s[...] = one_hot_s.astype(BF16)
            put_r[...] = one_hot_r.astype(BF16)
            loads[4].wait()
            loads[5].wait()
            pre[...] = dot(edges[...], w1[:d])

        late = me_r >= n_rcv // 2
        pl.when(jnp.logical_not(late))(prepare)

        pl.semaphore_wait(barrier, len(near) + len(greeted) + 1)
        for step in near:
            copy_plane(node_blk, me_r, plane(step)).start()
        for other in greeted:
            if other is two_columns:
                copy_turn(other, node_blk, me_s, 1).start()
            else:
                copy_snd(other, node_blk, nodes_s, 1).start()
        copy_sibling(node_blk, me_s).start()
        pl.when(late)(prepare)
        for step, passes in passed:
            block = plane(step)
            wait_plane(block)
            for to in passes:
                copy_plane(nodes_r.at[block], block, plane(to)).start()
            if step == 2:
                pltpu.make_async_copy(node_blk, nodes_s.at[two_columns], turn_sem).wait()
                copy_turn(two_lines, nodes_s.at[two_columns], two_columns, 0).start()

        wait_for(recv_sem, nodes_s, n_snd // 2 - 1, 1)
        for block in same_core:
            copy_sibling(nodes_s.at[block], block).start()
        wait_for(recv_sem, nodes_s, n_snd // 2 + 1, 0)
        receiver = dot(take_r[...], unpack_blocks(nodes_s[...]).astype(BF16)).astype(BF16)
        pre[...] += dot(receiver, w1[2 * d :])
        for step in (-1, 1, -4, 4, -5, 5, -6, 6, -7, 7, -8):
            wait_plane(plane(step))
        sender = dot(take_s[...], unpack_blocks(nodes_r[...]).astype(BF16)).astype(BF16)
        work[...] = dot(sender, w1[d : 2 * d])
        for start in range(0, n_edges, CHUNK):
            rows = pl.ds(start, CHUNK)
            act = pre[rows] + work[rows]
            pre[rows] = act
            hid[rows] = (act * jax.nn.sigmoid(act)).astype(BF16)
        loads[6].wait()
        work[...] = dot(hid[...], w2[...])
        for start in range(0, n_edges, CHUNK):
            rows = pl.ds(start, CHUNK)
            out, scale = layer_norm(work[rows])
            normed[rows] = out
            inv[rows] = scale
            hid[rows] = out.astype(BF16)
        agg_out[...] = pack_blocks(dot(put_r[...], hid[...]))
        send_snd(lambda o: agg_out.at[o], agg_in, 2)
        agg_in[me_s] = agg_out[me_s]

        loads[7].wait()
        loads[8].wait()
        loads[9].wait()
        loads[10].wait()
        node_pre = dot(nodes_ref[...], nw1[:d])
        for start in range(0, n_edges, CHUNK):
            rows = pl.ds(start, CHUNK)
            act = pre[rows]
            sigma = jax.nn.sigmoid(act)
            slope[rows] = sigma * (1.0 + act * (1.0 - sigma))

        wait_for(recv_sem, agg_in, n_snd, 2)
        aggregate = unpack_sum(agg_in[...]).astype(BF16)
        node_pre = node_pre + dot(aggregate, nw1[d:])
        sigma = jax.nn.sigmoid(node_pre)
        node_out = dot((node_pre * sigma).astype(BF16), nw2[...])
        node_normed, node_inv = layer_norm(node_out)
        gno = gno_ref[...].astype(F32)
        node_gout = norm_backward(gno, node_normed, node_inv).astype(BF16)
        node_gpre = (
            dot_t(node_gout, nw2[...]) * (sigma * (1.0 + node_pre * (1.0 - sigma)))
        ).astype(BF16)
        gagg = pack_blocks(dot_t(node_gpre, nw1[d:]))
        gagg_blk[...] = gagg[0]
        gagg_in[me_s] = gagg[0]
        send_snd(lambda o: gagg_blk, gagg_in, 3)
        direct = gno + dot_t(node_gpre, nw1[:d])

        wait_for(recv_sem, gagg_in, n_snd, 3)
        work[...] = dot(take_r[...], unpack_blocks(gagg_in[...]).astype(BF16))
        for start in range(0, n_edges, CHUNK):
            rows = pl.ds(start, CHUNK)
            live = (
                lax.broadcasted_iota(jnp.int32, (CHUNK, 1), 0) + start < count_ref[...]
            )
            up = work[rows] + jnp.where(live, geo[rows].astype(F32), 0.0)
            hid[rows] = norm_backward(up, normed[rows], inv[rows]).astype(BF16)
        work[...] = dot_t(hid[...], w2[...])
        for start in range(0, n_edges, CHUNK):
            rows = pl.ds(start, CHUNK)
            hid[rows] = (work[rows] * slope[rows]).astype(BF16)
        send_part = dot(put_s[...], hid[...]).astype(BF16)
        rs_out[...] = pack_blocks(dot_t(send_part, w1[d : 2 * d]))
        send_rcv(lambda o: rs_out.at[o], rs_in, 4)
        rs_in[me_r] = rs_out[me_r]
        recv_part = dot_t(hid[...], w1[2 * d :]).astype(BF16)
        rr_out[...] = pack_blocks(dot(put_r[...], recv_part))
        send_snd(lambda o: rr_out.at[o], rr_in, 5)
        rr_in[me_s] = rr_out[me_s]
        live_col = lax.broadcasted_iota(jnp.int32, (n_edges, 1), 0) < count_ref[...]
        gedges_ref[...] = jnp.where(live_col, geo[...].astype(F32), 0.0) + dot_t(
            hid[...], w1[:d]
        )

        wait_for(recv_sem, rr_in, n_snd, 5)
        direct = direct + unpack_sum(rr_in[...])
        wait_for(recv_sem, rs_in, n_rcv, 4)
        gnodes_ref[...] = direct + unpack_sum(rs_in[...])

        wait_for(send_sem, nodes_r, n_rcv, 0)
        wait_for(send_sem, nodes_s, n_snd, 1)
        wait_for(send_sem, agg_in, n_snd, 2)
        wait_for(send_sem, gagg_in, n_snd, 3)
        wait_for(send_sem, rs_in, n_rcv, 4)
        wait_for(send_sem, rr_in, n_snd, 5)

    return kernel


def solution(mesh):
    n_snd, n_rcv = mesh.shape["snd"], mesh.shape["rcv"]

    def local(
        nodes,
        edges,
        send_local,
        recv_local,
        edge_count,
        edge_w1,
        edge_w2,
        node_w1,
        node_w2,
        grad_nodes_out,
        grad_edges_out,
    ):
        n_edges, d = edges.shape[2:]
        vmem = pl.BlockSpec(memory_space=pltpu.VMEM)
        hbm = pl.BlockSpec(memory_space=pltpu.HBM)
        half = d // 2
        grad_nodes, grad_edges = pl.pallas_call(
            make_kernel(n_snd, n_rcv),
            out_shape=(
                pltpu.VMEM(nodes.shape, F32),
                pltpu.VMEM((n_edges, d), F32),
            ),
            in_specs=[hbm] * 11,
            out_specs=(vmem, vmem),
            scratch_shapes=[
                pltpu.VMEM((1, 1), jnp.int32),
                pltpu.VMEM((1, n_edges), jnp.int32),
                pltpu.VMEM((1, n_edges), jnp.int32),
                pltpu.VMEM(nodes.shape, BF16),
                pltpu.VMEM(nodes.shape, BF16),
                pltpu.VMEM((n_edges, d), BF16),
                pltpu.VMEM((n_edges, d), BF16),
                pltpu.VMEM(edge_w1.shape, BF16),
                pltpu.VMEM(edge_w2.shape, BF16),
                pltpu.VMEM(node_w1.shape, BF16),
                pltpu.VMEM(node_w2.shape, BF16),
                pltpu.VMEM((16, half), BF16),
                pltpu.VMEM((n_rcv, 16, half), BF16),
                pltpu.VMEM((n_snd, 16, half), BF16),
                pltpu.VMEM((n_snd, 16, half), BF16),
                pltpu.VMEM((n_snd, 16, half), BF16),
                pltpu.VMEM((16, half), BF16),
                pltpu.VMEM((n_snd, 16, half), BF16),
                pltpu.VMEM((n_rcv, 16, half), BF16),
                pltpu.VMEM((n_rcv, 16, half), BF16),
                pltpu.VMEM((n_snd, 16, half), BF16),
                pltpu.VMEM((n_snd, 16, half), BF16),
                pltpu.VMEM((n_edges, d), F32),
                pltpu.VMEM((n_edges, d), F32),
                pltpu.VMEM((n_edges, 1), F32),
                pltpu.VMEM((n_edges, d), F32),
                pltpu.VMEM((n_edges, d), BF16),
                pltpu.VMEM((n_edges, d), F32),
                pltpu.VMEM((n_rcv * 8, n_edges), BF16),
                pltpu.VMEM((n_snd * 8, n_edges), BF16),
                pltpu.VMEM((n_edges, n_rcv * 8), BF16),
                pltpu.VMEM((n_edges, n_snd * 8), BF16),
                pltpu.SemaphoreType.DMA((11,)),
                pltpu.SemaphoreType.DMA((6,)),
                pltpu.SemaphoreType.DMA((6,)),
                pltpu.SemaphoreType.DMA((n_rcv,)),
                pltpu.SemaphoreType.DMA,
            ],
            compiler_params=pltpu.CompilerParams(
                collective_id=0, has_side_effects=True, vmem_limit_bytes=48 * 1024 * 1024
            ),
        )(
            edge_count,
            *(
                pltpu.with_memory_space_constraint(operand, pltpu.HBM)
                for operand in (
                    send_local.reshape(1, n_edges),
                    recv_local.reshape(1, n_edges),
                    nodes,
                    grad_nodes_out,
                    edges.reshape(n_edges, d),
                    grad_edges_out.reshape(n_edges, d),
                    edge_w1,
                    edge_w2,
                    node_w1,
                    node_w2,
                )
            )
        )
        grad_nodes, grad_edges = hand_over(grad_nodes, grad_edges)
        return grad_nodes, grad_edges.reshape(1, 1, n_edges, d)

    in_specs = (
        P(("snd", "rcv"), None),
        P("snd", "rcv", None, None),
        P("snd", "rcv", None),
        P("snd", "rcv", None),
        P("snd", "rcv"),
        P(),
        P(),
        P(),
        P(),
        P(("snd", "rcv"), None),
        P("snd", "rcv", None, None),
    )
    out_specs = (P(("snd", "rcv"), None), P("snd", "rcv", None, None))
    return jax.shard_map(local, mesh=mesh, in_specs=in_specs, out_specs=out_specs, check_vma=False)
```

```python
import itertools

import jax
import jax.numpy as jnp
from jax import lax
from jax.experimental import pallas as pl
from jax.experimental.pallas import tpu as pltpu
from jax.sharding import PartitionSpec as P

MESH = pl.DeviceIdType.MESH
F32 = jnp.float32
BF16 = jnp.bfloat16
CHUNK = 64


def dot(a, b):
    return jnp.dot(a, b, preferred_element_type=F32)


def dot_t(a, b):
    return lax.dot_general(a, b, (((1,), (1,)), ((), ())), preferred_element_type=F32)


def pack_blocks(rows):
    count, width = rows.shape[0] // 8, rows.shape[1]
    blocks = rows.reshape(count, 8, width)
    return jnp.concatenate(
        [blocks[:, :, : width // 2], blocks[:, :, width // 2 :]], axis=1
    ).astype(BF16)


def unpack_blocks(blocks):
    blocks = blocks.astype(F32)
    count, _, half = blocks.shape
    return jnp.concatenate(
        [blocks[:, :8, :].reshape(count * 8, half), blocks[:, 8:, :].reshape(count * 8, half)],
        axis=1,
    )


def unpack_sum(blocks):
    total = jnp.sum(blocks.astype(F32), axis=0)
    return jnp.concatenate([total[:8], total[8:]], axis=1)


def layer_norm(values):
    center = values - jnp.mean(values, -1, keepdims=True)
    inv_scale = lax.rsqrt(jnp.mean(center * center, -1, keepdims=True) + 1e-05)
    return center * inv_scale, inv_scale


def norm_backward(upstream, normed, inv_scale):
    return inv_scale * (
        upstream
        - jnp.mean(upstream, -1, keepdims=True)
        - normed * jnp.mean(upstream * normed, -1, keepdims=True)
    )


def hand_over(grad_nodes, grad_edges):
    def kernel(nodes_in, edges_in, nodes_out, edges_out, sems):
        copies = [
            pltpu.make_async_copy(edges_in, edges_out, sems.at[0]),
            pltpu.make_async_copy(nodes_in, nodes_out, sems.at[1]),
        ]
        for copy in copies:
            copy.start()
        for copy in copies:
            copy.wait()

    vmem = pl.BlockSpec(memory_space=pltpu.VMEM)
    hbm = pl.BlockSpec(memory_space=pltpu.HBM)
    return pl.pallas_call(
        kernel,
        out_shape=(
            jax.ShapeDtypeStruct(grad_nodes.shape, F32),
            jax.ShapeDtypeStruct(grad_edges.shape, F32),
        ),
        in_specs=[vmem, vmem],
        out_specs=(hbm, hbm),
        scratch_shapes=[pltpu.SemaphoreType.DMA((2,))],
    )(
        pltpu.with_memory_space_constraint(grad_nodes, pltpu.VMEM),
        pltpu.with_memory_space_constraint(grad_edges, pltpu.VMEM),
    )


def make_kernel(n_snd, n_rcv):
    far_first = sorted(range(1, n_rcv), key=lambda step: -min(step, n_rcv - step))

    def kernel(
        count_hbm,
        send_hbm,
        recv_hbm,
        nodes_hbm,
        gno_hbm,
        edges_hbm,
        geo_hbm,
        w1_hbm,
        w2_hbm,
        nw1_hbm,
        nw2_hbm,
        gnodes_ref,
        gedges_ref,
        count_ref,
        send_ref,
        recv_ref,
        nodes_ref,
        gno_ref,
        edges,
        geo,
        w1,
        w2,
        nw1,
        nw2,
        node_blk,
        nodes_r,
        nodes_s,
        agg_out,
        agg_in,
        gagg_blk,
        gagg_in,
        rs_out,
        rs_in,
        rr_out,
        rr_in,
        pre,
        normed,
        inv,
        work,
        hid,
        slope,
        put_s,
        put_r,
        take_s,
        take_r,
        load_sem,
        send_sem,
        recv_sem,
        plane_sem,
        turn_sem,
    ):
        me_s = lax.axis_index("snd")
        me_r = lax.axis_index("rcv")
        n_edges = edges.shape[0]
        d = edges.shape[1]

        loads = [
            pltpu.make_async_copy(src, dst, load_sem.at[k])
            for k, (src, dst) in enumerate(
                [
                    (nodes_hbm, nodes_ref),
                    (count_hbm, count_ref),
                    (send_hbm, send_ref),
                    (recv_hbm, recv_ref),
                    (edges_hbm, edges),
                    (w1_hbm, w1),
                    (w2_hbm, w2),
                    (nw1_hbm, nw1),
                    (nw2_hbm, nw2),
                    (geo_hbm, geo),
                    (gno_hbm, gno_ref),
                ]
            )
        ]
        loads[0].start()

        barrier = pltpu.get_barrier_semaphore()

        def plane(step):
            return (me_r + step + n_rcv) % n_rcv

        cores = [me_s % 2, (me_s + 1) % 2]
        columns = [(me_s // 2 + dx) % 4 * 2 for dx in range(4)]
        lines = [(me_s // 8 + dy) % 4 * 8 for dy in range(4)]
        chips = sorted(
            itertools.product(range(4), range(4)),
            key=lambda step: -min(step[0], 4 - step[0]) - min(step[1], 4 - step[1]),
        )
        same_core, other_core = (
            [lines[dy] + columns[dx] + cores[core] for dy, dx in chips] for core in range(2)
        )
        same_core, sibling = same_core[:-1], other_core[-1]
        greeted = same_core[1:]
        two_lines, two_columns = (same_core[chips.index(chip)] for chip in ((2, 0), (0, 2)))
        snd_partners = other_core + same_core

        near = (3, -3, 2, -2, 1, -1)
        passed = ((-2, (2,)), (2, (-2,)), (-3, (5, 4, 3, 2)), (3, (-4, -3, -2)))
        for step in near:
            pl.semaphore_signal(
                barrier, inc=1, device_id={"rcv": plane(step)}, device_id_type=MESH
            )
        for other in greeted + [sibling]:
            pl.semaphore_signal(barrier, inc=1, device_id={"snd": other}, device_id_type=MESH)
        for load in loads[1:]:
            load.start()

        def copy_snd(other, src, dst, k):
            return pltpu.make_async_remote_copy(
                src_ref=src,
                dst_ref=dst.at[me_s],
                send_sem=send_sem.at[k],
                recv_sem=recv_sem.at[k],
                device_id={"snd": other},
                device_id_type=MESH,
            )

        def copy_turn(other, src, block, turn):
            return pltpu.make_async_remote_copy(
                src_ref=src,
                dst_ref=nodes_s.at[block],
                send_sem=send_sem.at[1],
                recv_sem=turn_sem if turn else recv_sem.at[1],
                device_id={"snd": other},
                device_id_type=MESH,
            )

        def copy_sibling(src, block):
            return pltpu.make_async_remote_copy(
                src_ref=src,
                dst_ref=nodes_s.at[block],
                send_sem=send_sem.at[1],
                recv_sem=recv_sem.at[0],
                device_id={"snd": sibling},
                device_id_type=MESH,
            )

        def send_snd(src_of, dst, k):
            for other in snd_partners:
                copy_snd(other, src_of(other), dst, k).start()

        def send_rcv(src_of, dst, k):
            for rank in range(n_rcv - 1):
                other = rank + jnp.where(rank >= me_r, 1, 0)
                pltpu.make_async_remote_copy(
                    src_ref=src_of(other),
                    dst_ref=dst.at[me_r],
                    send_sem=send_sem.at[k],
                    recv_sem=recv_sem.at[k],
                    device_id={"rcv": other},
                    device_id_type=MESH,
                ).start()

        def copy_plane(src, block, other):
            return pltpu.make_async_remote_copy(
                src_ref=src,
                dst_ref=nodes_r.at[block],
                send_sem=send_sem.at[0],
                recv_sem=plane_sem.at[block],
                device_id={"rcv": other},
                device_id_type=MESH,
            )

        def wait_plane(block):
            pltpu.make_async_copy(node_blk, nodes_r.at[block], plane_sem.at[block]).wait()

        def wait_for(sem, buf, n, k):
            part = buf.at[pl.ds(0, n - 1)]
            pltpu.make_async_copy(part, part, sem.at[k]).wait()

        loads[0].wait()
        own = pack_blocks(nodes_ref[...].astype(F32))
        node_blk[...] = own[0]
        nodes_r[me_r] = own[0]
        nodes_s[me_s] = own[0]

        def prepare():
            loads[1].wait()
            loads[2].wait()
            loads[3].wait()
            count = count_ref[...]
            live_row = lax.broadcasted_iota(jnp.int32, (1, n_edges), 1) < count
            send_idx = jnp.where(live_row, send_ref[...], -1)
            recv_idx = jnp.where(live_row, recv_ref[...], -1)

            def picker(idx, rows):
                rows_iota = lax.broadcasted_iota(jnp.int32, (rows, n_edges), 0)
                return jnp.where(rows_iota == idx, 1.0, 0.0).astype(F32)

            one_hot_s = picker(send_idx, n_rcv * 8)
            one_hot_r = picker(recv_idx, n_snd * 8)
            take_s[...] = one_hot_s.T.astype(BF16)
            take_r[...] = one_hot_r.T.astype(BF16)
            put_s[...] = one_hot_s.astype(BF16)
            put_r[...] = one_hot_r.astype(BF16)
            loads[4].wait()
            loads[5].wait()
            pre[...] = dot(edges[...], w1[:d])

        late = me_r >= n_rcv // 2
        pl.when(jnp.logical_not(late))(prepare)

        pl.semaphore_wait(barrier, len(near) + len(greeted) + 1)
        for step in near:
            copy_plane(node_blk, me_r, plane(step)).start()
        for other in greeted:
            if other is two_columns:
                copy_turn(other, node_blk, me_s, 1).start()
            else:
                copy_snd(other, node_blk, nodes_s, 1).start()
        copy_sibling(node_blk, me_s).start()
        pl.when(late)(prepare)
        for step, passes in passed:
            block = plane(step)
            wait_plane(block)
            for to in passes:
                copy_plane(nodes_r.at[block], block, plane(to)).start()
            if step == 2:
                pltpu.make_async_copy(node_blk, nodes_s.at[two_columns], turn_sem).wait()
                copy_turn(two_lines, nodes_s.at[two_columns], two_columns, 0).start()

        wait_for(recv_sem, nodes_s, n_snd // 2 - 1, 1)
        for block in same_core:
            copy_sibling(nodes_s.at[block], block).start()
        wait_for(recv_sem, nodes_s, n_snd // 2 + 1, 0)
        receiver = dot(take_r[...], unpack_blocks(nodes_s[...]).astype(BF16)).astype(BF16)
        pre[...] += dot(receiver, w1[2 * d :])
        for step in (-1, 1, -4, 4, -5, 5, -6, 6, -7, 7, -8):
            wait_plane(plane(step))
        sender = dot(take_s[...], unpack_blocks(nodes_r[...]).astype(BF16)).astype(BF16)
        work[...] = dot(sender, w1[d : 2 * d])
        for start in range(0, n_edges, CHUNK):
            rows = pl.ds(start, CHUNK)
            act = pre[rows] + work[rows]
            pre[rows] = act
            hid[rows] = (act * jax.nn.sigmoid(act)).astype(BF16)
        loads[6].wait()
        work[...] = dot(hid[...], w2[...])
        for start in range(0, n_edges, CHUNK):
            rows = pl.ds(start, CHUNK)
            out, scale = layer_norm(work[rows])
            normed[rows] = out
            inv[rows] = scale
            hid[rows] = out.astype(BF16)
        agg_out[...] = pack_blocks(dot(put_r[...], hid[...]))
        send_snd(lambda o: agg_out.at[o], agg_in, 2)
        agg_in[me_s] = agg_out[me_s]

        loads[7].wait()
        loads[8].wait()
        loads[9].wait()
        loads[10].wait()
        node_pre = dot(nodes_ref[...], nw1[:d])
        for start in range(0, n_edges, CHUNK):
            rows = pl.ds(start, CHUNK)
            act = pre[rows]
            sigma = jax.nn.sigmoid(act)
            slope[rows] = sigma * (1.0 + act * (1.0 - sigma))
        live_col = lax.broadcasted_iota(jnp.int32, (n_edges, 1), 0) < count_ref[...]
        gedges_ref[...] = jnp.where(live_col, geo[...].astype(F32), 0.0)

        wait_for(recv_sem, agg_in, n_snd, 2)
        aggregate = unpack_sum(agg_in[...]).astype(BF16)
        node_pre = node_pre + dot(aggregate, nw1[d:])
        sigma = jax.nn.sigmoid(node_pre)
        node_out = dot((node_pre * sigma).astype(BF16), nw2[...])
        node_normed, node_inv = layer_norm(node_out)
        gno = gno_ref[...].astype(F32)
        node_gout = norm_backward(gno, node_normed, node_inv).astype(BF16)
        node_gpre = (
            dot_t(node_gout, nw2[...]) * (sigma * (1.0 + node_pre * (1.0 - sigma)))
        ).astype(BF16)
        gagg = pack_blocks(dot_t(node_gpre, nw1[d:]))
        gagg_blk[...] = gagg[0]
        gagg_in[me_s] = gagg[0]
        send_snd(lambda o: gagg_blk, gagg_in, 3)
        direct = gno + dot_t(node_gpre, nw1[:d])

        wait_for(recv_sem, gagg_in, n_snd, 3)
        work[...] = dot(take_r[...], unpack_blocks(gagg_in[...]).astype(BF16))
        for start in range(0, n_edges, CHUNK):
            rows = pl.ds(start, CHUNK)
            up = work[rows] + gedges_ref[rows]
            hid[rows] = norm_backward(up, normed[rows], inv[rows]).astype(BF16)
        work[...] = dot_t(hid[...], w2[...])
        for start in range(0, n_edges, CHUNK):
            rows = pl.ds(start, CHUNK)
            hid[rows] = (work[rows] * slope[rows]).astype(BF16)
        send_part = dot(put_s[...], hid[...]).astype(BF16)
        rs_out[...] = pack_blocks(dot_t(send_part, w1[d : 2 * d]))
        send_rcv(lambda o: rs_out.at[o], rs_in, 4)
        rs_in[me_r] = rs_out[me_r]
        recv_part = dot_t(hid[...], w1[2 * d :]).astype(BF16)
        rr_out[...] = pack_blocks(dot(put_r[...], recv_part))
        send_snd(lambda o: rr_out.at[o], rr_in, 5)
        rr_in[me_s] = rr_out[me_s]
        gedges_ref[...] += dot_t(hid[...], w1[:d])

        wait_for(recv_sem, rr_in, n_snd, 5)
        direct = direct + unpack_sum(rr_in[...])
        wait_for(recv_sem, rs_in, n_rcv, 4)
        gnodes_ref[...] = direct + unpack_sum(rs_in[...])

        wait_for(send_sem, nodes_r, n_rcv, 0)
        wait_for(send_sem, nodes_s, n_snd, 1)
        wait_for(send_sem, agg_in, n_snd, 2)
        wait_for(send_sem, gagg_in, n_snd, 3)
        wait_for(send_sem, rs_in, n_rcv, 4)
        wait_for(send_sem, rr_in, n_snd, 5)

    return kernel


def solution(mesh):
    n_snd, n_rcv = mesh.shape["snd"], mesh.shape["rcv"]

    def local(
        nodes,
        edges,
        send_local,
        recv_local,
        edge_count,
        edge_w1,
        edge_w2,
        node_w1,
        node_w2,
        grad_nodes_out,
        grad_edges_out,
    ):
        n_edges, d = edges.shape[2:]
        vmem = pl.BlockSpec(memory_space=pltpu.VMEM)
        hbm = pl.BlockSpec(memory_space=pltpu.HBM)
        half = d // 2
        grad_nodes, grad_edges = pl.pallas_call(
            make_kernel(n_snd, n_rcv),
            out_shape=(
                pltpu.VMEM(nodes.shape, F32),
                pltpu.VMEM((n_edges, d), F32),
            ),
            in_specs=[hbm] * 11,
            out_specs=(vmem, vmem),
            scratch_shapes=[
                pltpu.VMEM((1, 1), jnp.int32),
                pltpu.VMEM((1, n_edges), jnp.int32),
                pltpu.VMEM((1, n_edges), jnp.int32),
                pltpu.VMEM(nodes.shape, BF16),
                pltpu.VMEM(nodes.shape, BF16),
                pltpu.VMEM((n_edges, d), BF16),
                pltpu.VMEM((n_edges, d), BF16),
                pltpu.VMEM(edge_w1.shape, BF16),
                pltpu.VMEM(edge_w2.shape, BF16),
                pltpu.VMEM(node_w1.shape, BF16),
                pltpu.VMEM(node_w2.shape, BF16),
                pltpu.VMEM((16, half), BF16),
                pltpu.VMEM((n_rcv, 16, half), BF16),
                pltpu.VMEM((n_snd, 16, half), BF16),
                pltpu.VMEM((n_snd, 16, half), BF16),
                pltpu.VMEM((n_snd, 16, half), BF16),
                pltpu.VMEM((16, half), BF16),
                pltpu.VMEM((n_snd, 16, half), BF16),
                pltpu.VMEM((n_rcv, 16, half), BF16),
                pltpu.VMEM((n_rcv, 16, half), BF16),
                pltpu.VMEM((n_snd, 16, half), BF16),
                pltpu.VMEM((n_snd, 16, half), BF16),
                pltpu.VMEM((n_edges, d), F32),
                pltpu.VMEM((n_edges, d), F32),
                pltpu.VMEM((n_edges, 1), F32),
                pltpu.VMEM((n_edges, d), F32),
                pltpu.VMEM((n_edges, d), BF16),
                pltpu.VMEM((n_edges, d), F32),
                pltpu.VMEM((n_rcv * 8, n_edges), BF16),
                pltpu.VMEM((n_snd * 8, n_edges), BF16),
                pltpu.VMEM((n_edges, n_rcv * 8), BF16),
                pltpu.VMEM((n_edges, n_snd * 8), BF16),
                pltpu.SemaphoreType.DMA((11,)),
                pltpu.SemaphoreType.DMA((6,)),
                pltpu.SemaphoreType.DMA((6,)),
                pltpu.SemaphoreType.DMA((n_rcv,)),
                pltpu.SemaphoreType.DMA,
            ],
            compiler_params=pltpu.CompilerParams(
                collective_id=0, has_side_effects=True, vmem_limit_bytes=48 * 1024 * 1024
            ),
        )(
            edge_count,
            *(
                pltpu.with_memory_space_constraint(operand, pltpu.HBM)
                for operand in (
                    send_local.reshape(1, n_edges),
                    recv_local.reshape(1, n_edges),
                    nodes,
                    grad_nodes_out,
                    edges.reshape(n_edges, d),
                    grad_edges_out.reshape(n_edges, d),
                    edge_w1,
                    edge_w2,
                    node_w1,
                    node_w2,
                )
            )
        )
        grad_nodes, grad_edges = hand_over(grad_nodes, grad_edges)
        return grad_nodes, grad_edges.reshape(1, 1, n_edges, d)

    in_specs = (
        P(("snd", "rcv"), None),
        P("snd", "rcv", None, None),
        P("snd", "rcv", None),
        P("snd", "rcv", None),
        P("snd", "rcv"),
        P(),
        P(),
        P(),
        P(),
        P(("snd", "rcv"), None),
        P("snd", "rcv", None, None),
    )
    out_specs = (P(("snd", "rcv"), None), P("snd", "rcv", None, None))
    return jax.shard_map(local, mesh=mesh, in_specs=in_specs, out_specs=out_specs, check_vma=False)
```

```python
import itertools

import jax
import jax.numpy as jnp
from jax import lax
from jax.experimental import pallas as pl
from jax.experimental.pallas import tpu as pltpu
from jax.sharding import PartitionSpec as P

MESH = pl.DeviceIdType.MESH
F32 = jnp.float32
BF16 = jnp.bfloat16
CHUNK = 64


def dot(a, b):
    return jnp.dot(a, b, preferred_element_type=F32)


def dot_t(a, b):
    return lax.dot_general(a, b, (((1,), (1,)), ((), ())), preferred_element_type=F32)


def pack_blocks(rows):
    count, width = rows.shape[0] // 8, rows.shape[1]
    blocks = rows.reshape(count, 8, width)
    return jnp.concatenate(
        [blocks[:, :, : width // 2], blocks[:, :, width // 2 :]], axis=1
    ).astype(BF16)


def unpack_blocks(blocks):
    blocks = blocks.astype(F32)
    count, _, half = blocks.shape
    return jnp.concatenate(
        [blocks[:, :8, :].reshape(count * 8, half), blocks[:, 8:, :].reshape(count * 8, half)],
        axis=1,
    )


def unpack_sum(blocks):
    total = jnp.sum(blocks.astype(F32), axis=0)
    return jnp.concatenate([total[:8], total[8:]], axis=1)


def layer_norm(values):
    center = values - jnp.mean(values, -1, keepdims=True)
    inv_scale = lax.rsqrt(jnp.mean(center * center, -1, keepdims=True) + 1e-05)
    return center * inv_scale, inv_scale


def norm_backward(upstream, normed, inv_scale):
    return inv_scale * (
        upstream
        - jnp.mean(upstream, -1, keepdims=True)
        - normed * jnp.mean(upstream * normed, -1, keepdims=True)
    )


def hand_over(grad_nodes, grad_edges):
    def kernel(nodes_in, edges_in, nodes_out, edges_out, sems):
        copies = [
            pltpu.make_async_copy(edges_in, edges_out, sems.at[0]),
            pltpu.make_async_copy(nodes_in, nodes_out, sems.at[1]),
        ]
        for copy in copies:
            copy.start()
        for copy in copies:
            copy.wait()

    vmem = pl.BlockSpec(memory_space=pltpu.VMEM)
    hbm = pl.BlockSpec(memory_space=pltpu.HBM)
    return pl.pallas_call(
        kernel,
        out_shape=(
            jax.ShapeDtypeStruct(grad_nodes.shape, F32),
            jax.ShapeDtypeStruct(grad_edges.shape, F32),
        ),
        in_specs=[vmem, vmem],
        out_specs=(hbm, hbm),
        scratch_shapes=[pltpu.SemaphoreType.DMA((2,))],
    )(
        pltpu.with_memory_space_constraint(grad_nodes, pltpu.VMEM),
        pltpu.with_memory_space_constraint(grad_edges, pltpu.VMEM),
    )


def make_kernel(n_snd, n_rcv):
    far_first = sorted(range(1, n_rcv), key=lambda step: -min(step, n_rcv - step))

    def kernel(
        count_hbm,
        send_hbm,
        recv_hbm,
        nodes_hbm,
        gno_hbm,
        edges_hbm,
        geo_hbm,
        w1_hbm,
        w2_hbm,
        nw1_hbm,
        nw2_hbm,
        gnodes_ref,
        gedges_ref,
        count_ref,
        send_ref,
        recv_ref,
        nodes_ref,
        gno_ref,
        edges,
        geo,
        w1,
        w2,
        nw1,
        nw2,
        node_blk,
        nodes_r,
        nodes_s,
        agg_out,
        agg_in,
        gagg_blk,
        gagg_in,
        rs_out,
        rs_in,
        rr_out,
        rr_in,
        pre,
        normed,
        inv,
        work,
        hid,
        slope,
        put_s,
        put_r,
        take_s,
        take_r,
        load_sem,
        send_sem,
        recv_sem,
        plane_sem,
        turn_sem,
    ):
        me_s = lax.axis_index("snd")
        me_r = lax.axis_index("rcv")
        n_edges = edges.shape[0]
        d = edges.shape[1]

        loads = [
            pltpu.make_async_copy(src, dst, load_sem.at[k])
            for k, (src, dst) in enumerate(
                [
                    (nodes_hbm, nodes_ref),
                    (count_hbm, count_ref),
                    (send_hbm, send_ref),
                    (recv_hbm, recv_ref),
                    (edges_hbm, edges),
                    (w1_hbm, w1),
                    (w2_hbm, w2),
                    (nw1_hbm, nw1),
                    (nw2_hbm, nw2),
                    (geo_hbm, geo),
                    (gno_hbm, gno_ref),
                ]
            )
        ]
        loads[0].start()

        barrier = pltpu.get_barrier_semaphore()

        def plane(step):
            return (me_r + step + n_rcv) % n_rcv

        cores = [me_s % 2, (me_s + 1) % 2]
        columns = [(me_s // 2 + dx) % 4 * 2 for dx in range(4)]
        lines = [(me_s // 8 + dy) % 4 * 8 for dy in range(4)]
        chips = sorted(
            itertools.product(range(4), range(4)),
            key=lambda step: -min(step[0], 4 - step[0]) - min(step[1], 4 - step[1]),
        )
        same_core, other_core = (
            [lines[dy] + columns[dx] + cores[core] for dy, dx in chips] for core in range(2)
        )
        same_core, sibling = same_core[:-1], other_core[-1]
        greeted = same_core[1:]
        two_lines, two_columns = (same_core[chips.index(chip)] for chip in ((2, 0), (0, 2)))
        snd_partners = other_core + same_core

        near = (3, -3, 2, -2, 1, -1)
        passed = ((-2, (2,)), (2, (-2,)), (-3, (4, 3, 2)), (3, (-4, -3, -2)))
        for step in near:
            pl.semaphore_signal(
                barrier, inc=1, device_id={"rcv": plane(step)}, device_id_type=MESH
            )
        for other in greeted + [sibling]:
            pl.semaphore_signal(barrier, inc=1, device_id={"snd": other}, device_id_type=MESH)
        for load in loads[1:]:
            load.start()

        def copy_snd(other, src, dst, k):
            return pltpu.make_async_remote_copy(
                src_ref=src,
                dst_ref=dst.at[me_s],
                send_sem=send_sem.at[k],
                recv_sem=recv_sem.at[k],
                device_id={"snd": other},
                device_id_type=MESH,
            )

        def copy_turn(other, src, block, turn):
            return pltpu.make_async_remote_copy(
                src_ref=src,
                dst_ref=nodes_s.at[block],
                send_sem=send_sem.at[1],
                recv_sem=turn_sem if turn else recv_sem.at[1],
                device_id={"snd": other},
                device_id_type=MESH,
            )

        def copy_sibling(src, block):
            return pltpu.make_async_remote_copy(
                src_ref=src,
                dst_ref=nodes_s.at[block],
                send_sem=send_sem.at[1],
                recv_sem=recv_sem.at[0],
                device_id={"snd": sibling},
                device_id_type=MESH,
            )

        def send_snd(src_of, dst, k):
            for other in snd_partners:
                copy_snd(other, src_of(other), dst, k).start()

        def send_rcv(src_of, dst, k):
            for rank in range(n_rcv - 1):
                other = rank + jnp.where(rank >= me_r, 1, 0)
                pltpu.make_async_remote_copy(
                    src_ref=src_of(other),
                    dst_ref=dst.at[me_r],
                    send_sem=send_sem.at[k],
                    recv_sem=recv_sem.at[k],
                    device_id={"rcv": other},
                    device_id_type=MESH,
                ).start()

        def copy_plane(src, block, other):
            return pltpu.make_async_remote_copy(
                src_ref=src,
                dst_ref=nodes_r.at[block],
                send_sem=send_sem.at[0],
                recv_sem=plane_sem.at[block],
                device_id={"rcv": other},
                device_id_type=MESH,
            )

        def wait_plane(block):
            pltpu.make_async_copy(node_blk, nodes_r.at[block], plane_sem.at[block]).wait()

        def wait_for(sem, buf, n, k):
            part = buf.at[pl.ds(0, n - 1)]
            pltpu.make_async_copy(part, part, sem.at[k]).wait()

        loads[0].wait()
        own = pack_blocks(nodes_ref[...].astype(F32))
        node_blk[...] = own[0]
        nodes_r[me_r] = own[0]
        nodes_s[me_s] = own[0]

        def prepare():
            loads[1].wait()
            loads[2].wait()
            loads[3].wait()
            count = count_ref[...]
            live_row = lax.broadcasted_iota(jnp.int32, (1, n_edges), 1) < count
            send_idx = jnp.where(live_row, send_ref[...], -1)
            recv_idx = jnp.where(live_row, recv_ref[...], -1)

            def picker(idx, rows):
                rows_iota = lax.broadcasted_iota(jnp.int32, (rows, n_edges), 0)
                return jnp.where(rows_iota == idx, 1.0, 0.0).astype(F32)

            one_hot_s = picker(send_idx, n_rcv * 8)
            one_hot_r = picker(recv_idx, n_snd * 8)
            take_s[...] = one_hot_s.T.astype(BF16)
            take_r[...] = one_hot_r.T.astype(BF16)
            put_s[...] = one_hot_s.astype(BF16)
            put_r[...] = one_hot_r.astype(BF16)
            loads[4].wait()
            loads[5].wait()
            pre[...] = dot(edges[...], w1[:d])

        late = me_r >= n_rcv // 2
        pl.when(jnp.logical_not(late))(prepare)

        pl.semaphore_wait(barrier, len(near) + len(greeted) + 1)
        for step in near:
            copy_plane(node_blk, me_r, plane(step)).start()
        for other in greeted:
            if other is two_columns:
                copy_turn(other, node_blk, me_s, 1).start()
            else:
                copy_snd(other, node_blk, nodes_s, 1).start()
        copy_sibling(node_blk, me_s).start()
        pl.when(late)(prepare)
        for step, passes in passed:
            block = plane(step)
            wait_plane(block)
            if step == 3:
                sign = 1 - 2 * (me_r % 2)
                far = plane(-3 * sign)
                copy_plane(nodes_r.at[far], far, plane(5 * sign)).start()
            for to in passes:
                copy_plane(nodes_r.at[block], block, plane(to)).start()
            if step == 2:
                pltpu.make_async_copy(node_blk, nodes_s.at[two_columns], turn_sem).wait()
                copy_turn(two_lines, nodes_s.at[two_columns], two_columns, 0).start()

        wait_for(recv_sem, nodes_s, n_snd // 2 - 1, 1)
        for block in same_core:
            copy_sibling(nodes_s.at[block], block).start()
        wait_for(recv_sem, nodes_s, n_snd // 2 + 1, 0)
        receiver = dot(take_r[...], unpack_blocks(nodes_s[...]).astype(BF16)).astype(BF16)
        pre[...] += dot(receiver, w1[2 * d :])
        for step in (-1, 1, -4, 4, -5, 5, -6, 6, -7, 7, -8):
            wait_plane(plane(step))
        sender = dot(take_s[...], unpack_blocks(nodes_r[...]).astype(BF16)).astype(BF16)
        work[...] = dot(sender, w1[d : 2 * d])
        for start in range(0, n_edges, CHUNK):
            rows = pl.ds(start, CHUNK)
            act = pre[rows] + work[rows]
            pre[rows] = act
            hid[rows] = (act * jax.nn.sigmoid(act)).astype(BF16)
        loads[6].wait()
        work[...] = dot(hid[...], w2[...])
        for start in range(0, n_edges, CHUNK):
            rows = pl.ds(start, CHUNK)
            out, scale = layer_norm(work[rows])
            normed[rows] = out
            inv[rows] = scale
            hid[rows] = out.astype(BF16)
        agg_out[...] = pack_blocks(dot(put_r[...], hid[...]))
        send_snd(lambda o: agg_out.at[o], agg_in, 2)
        agg_in[me_s] = agg_out[me_s]

        loads[7].wait()
        loads[8].wait()
        loads[9].wait()
        loads[10].wait()
        node_pre = dot(nodes_ref[...], nw1[:d])
        for start in range(0, n_edges, CHUNK):
            rows = pl.ds(start, CHUNK)
            act = pre[rows]
            sigma = jax.nn.sigmoid(act)
            slope[rows] = sigma * (1.0 + act * (1.0 - sigma))
        live_col = lax.broadcasted_iota(jnp.int32, (n_edges, 1), 0) < count_ref[...]
        gedges_ref[...] = jnp.where(live_col, geo[...].astype(F32), 0.0)

        wait_for(recv_sem, agg_in, n_snd, 2)
        aggregate = unpack_sum(agg_in[...]).astype(BF16)
        node_pre = node_pre + dot(aggregate, nw1[d:])
        sigma = jax.nn.sigmoid(node_pre)
        node_out = dot((node_pre * sigma).astype(BF16), nw2[...])
        node_normed, node_inv = layer_norm(node_out)
        gno = gno_ref[...].astype(F32)
        node_gout = norm_backward(gno, node_normed, node_inv).astype(BF16)
        node_gpre = (
            dot_t(node_gout, nw2[...]) * (sigma * (1.0 + node_pre * (1.0 - sigma)))
        ).astype(BF16)
        gagg = pack_blocks(dot_t(node_gpre, nw1[d:]))
        gagg_blk[...] = gagg[0]
        gagg_in[me_s] = gagg[0]
        send_snd(lambda o: gagg_blk, gagg_in, 3)
        direct = gno + dot_t(node_gpre, nw1[:d])

        wait_for(recv_sem, gagg_in, n_snd, 3)
        work[...] = dot(take_r[...], unpack_blocks(gagg_in[...]).astype(BF16))
        for start in range(0, n_edges, CHUNK):
            rows = pl.ds(start, CHUNK)
            up = work[rows] + gedges_ref[rows]
            hid[rows] = norm_backward(up, normed[rows], inv[rows]).astype(BF16)
        work[...] = dot_t(hid[...], w2[...])
        for start in range(0, n_edges, CHUNK):
            rows = pl.ds(start, CHUNK)
            hid[rows] = (work[rows] * slope[rows]).astype(BF16)
        send_part = dot(put_s[...], hid[...]).astype(BF16)
        rs_out[...] = pack_blocks(dot_t(send_part, w1[d : 2 * d]))
        send_rcv(lambda o: rs_out.at[o], rs_in, 4)
        rs_in[me_r] = rs_out[me_r]
        recv_part = dot_t(hid[...], w1[2 * d :]).astype(BF16)
        rr_out[...] = pack_blocks(dot(put_r[...], recv_part))
        send_snd(lambda o: rr_out.at[o], rr_in, 5)
        rr_in[me_s] = rr_out[me_s]
        gedges_ref[...] += dot_t(hid[...], w1[:d])

        wait_for(recv_sem, rr_in, n_snd, 5)
        direct = direct + unpack_sum(rr_in[...])
        wait_for(recv_sem, rs_in, n_rcv, 4)
        gnodes_ref[...] = direct + unpack_sum(rs_in[...])

        wait_for(send_sem, nodes_r, n_rcv, 0)
        wait_for(send_sem, nodes_s, n_snd, 1)
        wait_for(send_sem, agg_in, n_snd, 2)
        wait_for(send_sem, gagg_in, n_snd, 3)
        wait_for(send_sem, rs_in, n_rcv, 4)
        wait_for(send_sem, rr_in, n_snd, 5)

    return kernel


def solution(mesh):
    n_snd, n_rcv = mesh.shape["snd"], mesh.shape["rcv"]

    def local(
        nodes,
        edges,
        send_local,
        recv_local,
        edge_count,
        edge_w1,
        edge_w2,
        node_w1,
        node_w2,
        grad_nodes_out,
        grad_edges_out,
    ):
        n_edges, d = edges.shape[2:]
        vmem = pl.BlockSpec(memory_space=pltpu.VMEM)
        hbm = pl.BlockSpec(memory_space=pltpu.HBM)
        half = d // 2
        grad_nodes, grad_edges = pl.pallas_call(
            make_kernel(n_snd, n_rcv),
            out_shape=(
                pltpu.VMEM(nodes.shape, F32),
                pltpu.VMEM((n_edges, d), F32),
            ),
            in_specs=[hbm] * 11,
            out_specs=(vmem, vmem),
            scratch_shapes=[
                pltpu.VMEM((1, 1), jnp.int32),
                pltpu.VMEM((1, n_edges), jnp.int32),
                pltpu.VMEM((1, n_edges), jnp.int32),
                pltpu.VMEM(nodes.shape, BF16),
                pltpu.VMEM(nodes.shape, BF16),
                pltpu.VMEM((n_edges, d), BF16),
                pltpu.VMEM((n_edges, d), BF16),
                pltpu.VMEM(edge_w1.shape, BF16),
                pltpu.VMEM(edge_w2.shape, BF16),
                pltpu.VMEM(node_w1.shape, BF16),
                pltpu.VMEM(node_w2.shape, BF16),
                pltpu.VMEM((16, half), BF16),
                pltpu.VMEM((n_rcv, 16, half), BF16),
                pltpu.VMEM((n_snd, 16, half), BF16),
                pltpu.VMEM((n_snd, 16, half), BF16),
                pltpu.VMEM((n_snd, 16, half), BF16),
                pltpu.VMEM((16, half), BF16),
                pltpu.VMEM((n_snd, 16, half), BF16),
                pltpu.VMEM((n_rcv, 16, half), BF16),
                pltpu.VMEM((n_rcv, 16, half), BF16),
                pltpu.VMEM((n_snd, 16, half), BF16),
                pltpu.VMEM((n_snd, 16, half), BF16),
                pltpu.VMEM((n_edges, d), F32),
                pltpu.VMEM((n_edges, d), F32),
                pltpu.VMEM((n_edges, 1), F32),
                pltpu.VMEM((n_edges, d), F32),
                pltpu.VMEM((n_edges, d), BF16),
                pltpu.VMEM((n_edges, d), F32),
                pltpu.VMEM((n_rcv * 8, n_edges), BF16),
                pltpu.VMEM((n_snd * 8, n_edges), BF16),
                pltpu.VMEM((n_edges, n_rcv * 8), BF16),
                pltpu.VMEM((n_edges, n_snd * 8), BF16),
                pltpu.SemaphoreType.DMA((11,)),
                pltpu.SemaphoreType.DMA((6,)),
                pltpu.SemaphoreType.DMA((6,)),
                pltpu.SemaphoreType.DMA((n_rcv,)),
                pltpu.SemaphoreType.DMA,
            ],
            compiler_params=pltpu.CompilerParams(
                collective_id=0, has_side_effects=True, vmem_limit_bytes=48 * 1024 * 1024
            ),
        )(
            edge_count,
            *(
                pltpu.with_memory_space_constraint(operand, pltpu.HBM)
                for operand in (
                    send_local.reshape(1, n_edges),
                    recv_local.reshape(1, n_edges),
                    nodes,
                    grad_nodes_out,
                    edges.reshape(n_edges, d),
                    grad_edges_out.reshape(n_edges, d),
                    edge_w1,
                    edge_w2,
                    node_w1,
                    node_w2,
                )
            )
        )
        grad_nodes, grad_edges = hand_over(grad_nodes, grad_edges)
        return grad_nodes, grad_edges.reshape(1, 1, n_edges, d)

    in_specs = (
        P(("snd", "rcv"), None),
        P("snd", "rcv", None, None),
        P("snd", "rcv", None),
        P("snd", "rcv", None),
        P("snd", "rcv"),
        P(),
        P(),
        P(),
        P(),
        P(("snd", "rcv"), None),
        P("snd", "rcv", None, None),
    )
    out_specs = (P(("snd", "rcv"), None), P("snd", "rcv", None, None))
    return jax.shard_map(local, mesh=mesh, in_specs=in_specs, out_specs=out_specs, check_vma=False)
```
